512 devices in a mesh: dp: 32 (over y, x_hi, core), expert: 16 (over z, x_lo).
Axes of the slice: x: 4 (x_hi: 2, x_lo: 2; x = x_hi * 2 + x_lo), y: 8, z: 8, core: 2. Of those that a mesh axis runs over, the one named last changes fastest.
Arguments:
- tokens: bfloat16 [65536, 1280], P(('dp', 'expert')), may hold values from -24 to 24
- out_grad: bfloat16 [65536, 1280], P(('dp', 'expert')), may hold values from -9 to 9
- routes: int32 [65536, 8], P(('dp', 'expert')), may hold values from 0 to 127, as said below
- gate_values: bfloat16 [65536, 8], P(('dp', 'expert')), may hold values from 0.029907227 to 0.3984375
- w_gate: bfloat16 [16, 1280, 512], P('expert', 'dp'), may hold values from -0.15625 to 0.15625
- w_up: bfloat16 [16, 1280, 512], P('expert', 'dp'), may hold values from -0.15625 to 0.15625
- w_down: bfloat16 [16, 512, 1280], P('expert', 'dp'), may hold values from -0.25 to 0.25
Outputs:
- token_grad: bfloat16 [65536, 1280], P(('dp', 'expert'))
- gate_grad: bfloat16 [65536, 8], P(('dp', 'expert'))
- w_gate_grad: bfloat16 [16, 1280, 512], P('expert', 'dp')
- w_up_grad: bfloat16 [16, 1280, 512], P('expert', 'dp')
- w_down_grad: bfloat16 [16, 512, 1280], P('expert', 'dp')
The draws below stay inside these ranges and needn't reach their ends.
Inputs may be any that keep to these rules, and one draw needn't show every extreme that they name: `routes`: each row names 8 different experts. Among the 128 rows of one device (aligned blocks), no expert whose number is a multiple of 8 is named by more than 16 rows, and each row names at most two such experts.
All inputs are finite; a program needn't handle non-finite values.
Results may differ from the reference program's by a relative error of at most 0.02.
Values may be sent and summed in bfloat16 or wider, within the bound.
A program may use at most 64 MiB of HBM per device.

```python
import math
import jax
import jax.numpy as jnp
from jax import lax

D = 1280
FF = 512
TOP = 8
EXP_DEV = 8
TOK_DEV = 128
EXPERTS = 128
CAP = 16
TOKENS = 65536
N_DP = 32
N_EXPERT = 16


def draw_routes(key, part):
    key = jax.random.fold_in(key, 17)
    subkeys = jax.random.split(key, 7)
    blocks = N_DP * N_EXPERT
    half_count = N_EXPERT // 2
    favoured = jnp.repeat(jax.random.randint(subkeys[0], (N_DP,), 0, N_EXPERT), N_EXPERT)
    flight = jnp.arange(N_EXPERT, dtype=jnp.int32)[None, :]
    order_score = jax.random.randint(subkeys[1], (blocks, N_EXPERT), 0, 65536) * N_EXPERT + flight
    order_score = jnp.where(flight == favoured[:, None], -1, order_score)
    flight_order = jnp.argsort(order_score, axis=1).astype(jnp.int32)
    token_pos = jnp.arange(TOK_DEV, dtype=jnp.int32)
    place_score = jax.random.randint(subkeys[2], (blocks, 2, TOK_DEV), 0, 65536) * TOK_DEV + token_pos
    place_rank = jnp.argsort(jnp.argsort(place_score, axis=2), axis=2).astype(jnp.int32)
    column_slot = place_rank // CAP + jnp.array([0, half_count], dtype=jnp.int32)[None, :, None]
    picked = jnp.take_along_axis(flight_order, column_slot.reshape(blocks, 2 * TOK_DEV), axis=1)
    levels = jax.random.randint(subkeys[3], (blocks, N_EXPERT), 1, 6)
    levels = jnp.where(flight == favoured[:, None], 8, levels)
    picked_level = jnp.take_along_axis(levels, picked, axis=1).reshape(blocks, 2, TOK_DEV)
    picked = picked.reshape(blocks, 2, TOK_DEV)
    retained = jax.random.randint(subkeys[4], (blocks, 2, TOK_DEV), 0, 8) < picked_level
    flight_ids = picked * EXP_DEV
    all_ids = jnp.arange(EXPERTS, dtype=jnp.int32)
    fill_score = jax.random.randint(subkeys[5], (blocks, TOK_DEV, EXPERTS), 0, 65536) * EXPERTS + all_ids
    fill_score = jnp.where(all_ids % EXP_DEV == 0, -1, fill_score)
    fillers = lax.top_k(fill_score, TOP)[1].astype(jnp.int32)
    first_col = jnp.where(retained[:, 0, :], flight_ids[:, 0, :], fillers[:, :, 0])
    second = jnp.where(retained[:, 1, :], flight_ids[:, 1, :], fillers[:, :, 1])
    columns = jnp.concatenate([first_col[:, :, None], second[:, :, None], fillers[:, :, 2:]], axis=2)
    shuffle = jax.random.randint(subkeys[6], (blocks, TOK_DEV, TOP), 0, 65536) * TOP + jnp.arange(TOP, dtype=jnp.int32)
    shuffled_order = jnp.argsort(shuffle, axis=2)
    return jnp.take_along_axis(columns, shuffled_order, axis=2).reshape(TOKENS, TOP).astype(jnp.int32)


def raised(result, own_key, source, target, blocks, factor):
    owner, partner = [(jnp.arange(result.shape[dim]) // (result.shape[dim] // blocks)).reshape([-1 if axis == dim else 1 for axis in range(result.ndim)]) for dim in (source, target)]
    chosen = jax.random.permutation(own_key, blocks)[partner]
    strong = (owner == chosen) | (owner == (partner + blocks // 2) % blocks)
    return jnp.where(strong, factor * result, result)


def steps_of(stream_key, shape, shards, smallest, largest):
    def one(axis_at, parts):
        heights = jax.random.uniform(jax.random.fold_in(jax.random.fold_in(stream_key, 6), axis_at), (parts,), jnp.float32, smallest / len(shards), largest / len(shards))
        return jnp.repeat(jnp.exp(heights), shape[axis_at] // parts).reshape((-1,) + (1,) * (len(shape) - axis_at - 1))

    gain = one(*shards[0])
    for cut in shards[1:]:
        gain = gain * one(*cut)
    return gain


def normal_values(stream_key, dims, scale, most, shards=(), held_as=jnp.bfloat16):
    result = jax.random.normal(stream_key, dims, jnp.float32) * scale
    if len(shards) > 0:
        result = steps_of(stream_key, dims, shards, -0.22, 0.18) * result
    return jnp.clip(result, min=-most, max=most).astype(held_as)


def gaussian_with(own_key, shape, scale, most, cuts, heavy, kind=jnp.bfloat16):
    result = scale * jax.random.normal(own_key, shape, jnp.float32)
    if cuts:
        result = result * steps_of(own_key, shape, cuts, -0.22, 0.18)
    return jnp.clip(raised(result, jax.random.fold_in(own_key, 3), *heavy), -most, most).astype(kind)


def setup_inputs(seed: int = 0) -> dict:
    key_list = jax.random.split(jax.random.key(seed), 8)
    tokens = gaussian_with(key_list[0], (TOKENS, D), 1.0, 24.0, ((0, 512),), (0, 1, 256, 6.0))
    out_grad = normal_values(key_list[1], (TOKENS, D), 1.5, 9.0, ((0, 512),))
    routes = draw_routes(jax.random.fold_in(key_list[7], 71), 0)
    gate_values = jnp.clip(jnp.exp(math.log(0.3984375) - 2.5894505 * jax.random.uniform(key_list[3], (TOKENS, TOP), jnp.float32) ** steps_of(key_list[3], (TOKENS, TOP), ((0, 512),), -0.2, 0.2)), 0.029907227, 0.3984375).astype(jnp.bfloat16)
    w_gate = normal_values(key_list[4], (N_EXPERT, D, FF), D ** -0.5, 0.15625, ((0, 16), (1, 32)))
    w_up = normal_values(key_list[5], (N_EXPERT, D, FF), D ** -0.5, 0.15625, ((0, 16), (1, 32)))
    w_down = normal_values(key_list[6], (N_EXPERT, FF, D), FF ** -0.5, 0.25, ((0, 16), (1, 32)))
    return {"tokens": tokens, "out_grad": out_grad, "routes": routes, "gate_values": gate_values, "w_gate": w_gate, "w_up": w_up, "w_down": w_down}


CONTRACT_LAST = (((1,), (1,)), ((), ()))


def expert_pass(inputs, grad_rows, gate_col, full_gate, full_up, full_down):
    gate_pre = jnp.dot(inputs, full_gate, preferred_element_type=jnp.float32)
    up_pre = jnp.dot(inputs, full_up, preferred_element_type=jnp.float32)
    squash = jax.nn.sigmoid(gate_pre)
    activation = (gate_pre * squash * up_pre).astype(jnp.bfloat16)
    expert_out = jnp.dot(activation, full_down, preferred_element_type=jnp.float32)
    grad_wide = grad_rows.astype(jnp.float32)
    gate_term = jnp.sum(grad_wide * expert_out, axis=1).astype(jnp.bfloat16)
    scaled_grad = (gate_col * grad_wide).astype(jnp.bfloat16)
    act_grad = lax.dot_general(scaled_grad, full_down, CONTRACT_LAST, preferred_element_type=jnp.float32)
    pre_gate = (act_grad * up_pre * squash * (1.0 + gate_pre * (1.0 - squash))).astype(jnp.bfloat16)
    pre_up = (act_grad * gate_pre * squash).astype(jnp.bfloat16)
    input_grad = (lax.dot_general(pre_gate, full_gate, CONTRACT_LAST, preferred_element_type=jnp.float32)
                  + lax.dot_general(pre_up, full_up, CONTRACT_LAST, preferred_element_type=jnp.float32)).astype(jnp.bfloat16)
    return input_grad, gate_term, pre_gate, pre_up, activation, scaled_grad


def reference(tokens, out_grad, routes, gate_values, w_gate, w_up, w_down):
    blocks = N_DP * N_EXPERT
    inputs_all = tokens.reshape(blocks, TOK_DEV, D)
    grads_all = out_grad.reshape(blocks, TOK_DEV, D)
    routes_all = routes.reshape(blocks, TOK_DEV, TOP)
    gates_all = gate_values.reshape(blocks, TOK_DEV, TOP).astype(jnp.float32)
    block_index = jnp.arange(blocks, dtype=jnp.int32)[:, None]

    def one_expert(totals, expert_pos):
        token_acc, gate_acc = totals
        full_gate = lax.dynamic_index_in_dim(w_gate, expert_pos, 0, keepdims=False)
        full_up = lax.dynamic_index_in_dim(w_up, expert_pos, 0, keepdims=False)
        full_down = lax.dynamic_index_in_dim(w_down, expert_pos, 0, keepdims=False)
        matched = routes_all == expert_pos * EXP_DEV
        chosen = jnp.any(matched, axis=2)
        gate_tok = jnp.sum(jnp.where(matched, gates_all, 0.0), axis=2)
        slot_order = jnp.argsort(jnp.where(chosen, 0, 1).astype(jnp.int32), axis=1)[:, :CAP].astype(jnp.int32)
        filled = jnp.take_along_axis(chosen, slot_order, axis=1)
        picked_in = jnp.take_along_axis(inputs_all, slot_order[:, :, None], axis=1)
        picked_in = jnp.where(filled[:, :, None], picked_in, jnp.zeros((), jnp.bfloat16))
        picked_grad = jnp.take_along_axis(grads_all, slot_order[:, :, None], axis=1)
        picked_grad = jnp.where(filled[:, :, None], picked_grad, jnp.zeros((), jnp.bfloat16))
        gate_col = jnp.where(filled, jnp.take_along_axis(gate_tok, slot_order, axis=1), 0.0).reshape(-1, 1)
        inputs = picked_in.reshape(-1, D)
        grad_rows = picked_grad.reshape(-1, D)
        input_grad, gate_term, pre_gate, pre_up, activation, scaled_grad = expert_pass(
            inputs, grad_rows, gate_col, full_gate, full_up, full_down)
        stacked = jnp.concatenate([pre_gate, pre_up], axis=1).reshape(N_DP, -1, 2 * FF).astype(jnp.float32)
        grouped_in = inputs.reshape(N_DP, -1, D).astype(jnp.float32)
        partials = jnp.einsum("grd,grh->gdh", grouped_in, stacked)
        partials = lax.optimization_barrier(partials.astype(jnp.bfloat16))
        gate_up_sum = jnp.sum(partials.astype(jnp.float32), axis=0).astype(jnp.bfloat16)
        grouped_act = activation.reshape(N_DP, -1, FF).astype(jnp.float32)
        grouped_scaled = scaled_grad.reshape(N_DP, -1, D).astype(jnp.float32)
        down_parts = jnp.einsum("grh,grd->ghd", grouped_act, grouped_scaled)
        down_parts = lax.optimization_barrier(down_parts.astype(jnp.bfloat16))
        down_sum = jnp.sum(down_parts.astype(jnp.float32), axis=0).astype(jnp.bfloat16)
        back_rows = jnp.where(filled[:, :, None], input_grad.reshape(blocks, CAP, D).astype(jnp.float32), 0.0)
        token_acc = token_acc.at[block_index, slot_order].add(back_rows)
        gate_vals = jnp.where(filled, gate_term.reshape(blocks, CAP).astype(jnp.float32), 0.0)
        gate_by = jnp.zeros((blocks, TOK_DEV), jnp.float32).at[block_index, slot_order].add(gate_vals)
        gate_acc = gate_acc + jnp.where(matched, gate_by[:, :, None], 0.0)
        return (token_acc, gate_acc), (gate_up_sum, down_sum)

    start = (jnp.zeros((blocks, TOK_DEV, D), jnp.float32), jnp.zeros((blocks, TOK_DEV, TOP), jnp.float32))
    finals, stacked_out = lax.scan(one_expert, start, jnp.arange(N_EXPERT, dtype=jnp.int32))
    gate_up_all, down_all = stacked_out
    token_grad = finals[0].astype(jnp.bfloat16).reshape(TOKENS, D)
    gate_grad = finals[1].astype(jnp.bfloat16).reshape(TOKENS, TOP)
    return token_grad, gate_grad, gate_up_all[:, :, :FF], gate_up_all[:, :, FF:], down_all
```

```python
import jax
import jax.numpy as jnp
from jax import lax
from jax.experimental import pallas as pl
from jax.experimental.pallas import tpu as pltpu
from jax.sharding import PartitionSpec as P

EXP_DEV = 8
MESH = pl.DeviceIdType.MESH
BF = jnp.bfloat16
F32 = jnp.float32
ROWS = (((0,), (0,)), ((), ()))
LAST = (((1,), (1,)), ((), ()))

N_E = 16
N_Y = 8
TOK = 128
CAP = 16
SLOTS = N_E * CAP
D = 1280
FF = 512
WIDE = D + 128
UNIT = 80
HALF = 40
DOWN = 16
STEPS = ((4, 3), (3, 4))


def kernel(
    tokens, grads, routes, gates, wg, wu, wd,
    tok_out, gate_out, wg_out, wu_out, wd_out,
    place_ref, send_x, send_g, got_x, got_g, ret, back,
    w_own, w_sib, w2, wdn,
    h_ref, u_ref, g_ref, a_ref, dhu_ref, e_ref,
    d2, dd, s2, sd, snd2, sndd, rec2, recd, xs2, xsd, xr2, xrd, cs, cr,
    sx, rx, sg, rg, sr, rr, s0, r0, sxw, rxw, sag, rag, ssw, rsw,
    ssd, rsd, srs, rrs, sxr, rxr, scr, rcr,
):
    dp = lax.axis_index("dp")
    ex = lax.axis_index("expert")
    core = lax.rem(dp, 2)
    xh = lax.rem(lax.div(dp, 2), 2)
    y = lax.div(dp, 4)
    other = 1 - core
    low = lax.rem(dp, 4)
    sibling = (dp + 1 - 2 * core, ex)
    partner = (dp + 2 - 4 * xh, ex)
    ups = (
        (lax.rem(y + 1, N_Y) * 4 + low, ex),
        (lax.rem(y + N_Y - 1, N_Y) * 4 + low, ex),
    )

    def wrap(offset):
        return lax.rem(y + (offset + 2 * N_Y), N_Y)

    def peer(k):
        return lax.rem(ex + (k + N_E), N_E)

    def remote(src, dst, send, recv, to):
        return pltpu.make_async_remote_copy(
            src_ref=src, dst_ref=dst, send_sem=send, recv_sem=recv,
            device_id=to, device_id_type=MESH,
        )

    started = []

    def go(*args):
        copy = remote(*args)
        copy.start()
        started.append(copy)
        return copy

    barrier = pltpu.get_barrier_semaphore()
    for to in (sibling, partner) + ups:
        pl.semaphore_signal(barrier, inc=1, device_id=to, device_id_type=MESH)
    for k in range(1, N_E):
        pl.semaphore_signal(barrier, inc=1, device_id=(dp, peer(k)), device_id_type=MESH)

    lane = lax.broadcasted_iota(jnp.int32, (TOK, SLOTS), 1)
    expert_id = lax.div(lane, CAP) * EXP_DEV
    slot_id = lax.rem(lane, CAP)
    route = routes[...]
    gate_wide = gates[...].astype(F32)
    chosen = jnp.zeros((TOK, SLOTS), F32)
    gate_tok = jnp.zeros((TOK, SLOTS), F32)
    for k in range(8):
        match = route[:, k : k + 1] == expert_id
        chosen = jnp.where(match, 1.0, chosen)
        gate_tok = jnp.where(match, gate_wide[:, k : k + 1], gate_tok)
    before = (
        lax.broadcasted_iota(jnp.int32, (TOK, TOK), 0)
        > lax.broadcasted_iota(jnp.int32, (TOK, TOK), 1)
    )
    before = jnp.where(before, 1.0, 0.0).astype(BF)
    rank = jnp.dot(before, chosen.astype(BF), preferred_element_type=F32)
    placing = jnp.where(rank == slot_id.astype(F32), chosen, 0.0)
    gate_slot = (placing * gate_tok).astype(BF)
    placing = placing.astype(BF)
    place_ref[...] = placing
    w_own[0] = wg[...]
    w_own[1] = wu[...]
    wdn[y, xh, core] = wd[...]
    send_x[...] = (
        lax.dot_general(placing, tokens[...], ROWS, preferred_element_type=F32)
        .astype(BF).reshape(N_E, CAP, D)
    )

    pl.semaphore_wait(barrier, 4 + N_E - 1)

    first = go(w_own.at[other], w_sib, s0, r0, sibling)
    part_d = go(wdn.at[y, xh, core], wdn.at[y, xh, core], sxw.at[1], rxw.at[1], partner)
    row_x = [
        go(send_x.at[peer(k)], got_x.at[ex], sx.at[k], rx.at[k], (dp, peer(k)))
        for k in range(1, N_E)
    ]
    got_x[ex] = send_x[ex]

    first.wait_recv()
    mine = w_own[core].astype(F32)
    theirs = w_sib[...].astype(F32)
    is_first = core == 0
    w2[core, 2 * y + xh] = jnp.concatenate(
        [jnp.where(is_first, mine, theirs), jnp.where(is_first, theirs, mine)], axis=0
    ).astype(BF)
    part_2 = go(
        w2.at[core, 2 * y + xh], w2.at[core, 2 * y + xh], sxw.at[0], rxw.at[0], partner
    )

    send_g[:, :, :D] = (
        lax.dot_general(placing, grads[...], ROWS, preferred_element_type=F32)
        .astype(BF).reshape(N_E, CAP, D)
    )
    send_g[:, :, D:] = (
        lax.dot_general(gate_slot, jnp.ones((TOK, 128), BF), ROWS, preferred_element_type=F32)
        .astype(BF).reshape(N_E, CAP, 128)
    )
    got_g[ex] = send_g[ex]

    def block(piece, at):
        if piece == 0:
            return w2.at[core, pl.ds(2 * at, 2)]
        return wdn.at[at, :, core]

    def ring_send(piece, way, step):
        at = block(piece, wrap(-step if way == 0 else step))
        return go(at, at, sag.at[piece, way, step], rag.at[piece, way, step], ups[way])

    def to_sibling(piece, at, index):
        at = block(piece, at)
        return go(at, at, ssw.at[piece, index], rsw.at[piece, index], sibling)

    part_d.wait_recv()
    part_2.wait_recv()
    ring = {}
    shared = []
    for piece in range(2):
        for way in range(2):
            ring[piece, way] = ring_send(piece, way, 0)
    row_g = [
        go(send_g.at[peer(k)], got_g.at[ex], sg.at[k], rg.at[k], (dp, peer(k)))
        for k in range(1, N_E)
    ]
    for piece in range(2):
        shared.append(to_sibling(piece, y, 0))
    for step in range(4):
        for piece in range(2):
            for way in range(2):
                if step < STEPS[piece][way]:
                    ring[piece, way].wait_recv()
                    if step + 1 < STEPS[piece][way]:
                        ring[piece, way] = ring_send(piece, way, step + 1)
                    offset = -1 - step if way == 0 else 1 + step
                    index = 1 + step if way == 0 else 1 + STEPS[piece][0] + step
                    shared.append(to_sibling(piece, wrap(offset), index))
    for copy in shared:
        copy.wait_recv()
    for copy in row_x:
        copy.wait_recv()

    rows = got_x[...].reshape(SLOTS, D)
    h_ref[...] = jnp.dot(rows, w2[0].reshape(D, FF), preferred_element_type=F32)
    u_ref[...] = jnp.dot(rows, w2[1].reshape(D, FF), preferred_element_type=F32)
    for copy in row_g:
        copy.wait_recv()
    g_ref[...] = lax.dot_general(
        got_g[:, :, :D].reshape(SLOTS, D), wdn[...].reshape(FF, D), LAST,
        preferred_element_type=F32,
    )

    def elementwise(i, carry):
        at = pl.ds(pl.multiple_of(i * CAP, CAP), CAP)
        h, u, g = h_ref[at], u_ref[at], g_ref[at]
        row = got_g[i]
        gate = row[:, D : D + 1].astype(F32)
        s = jax.nn.sigmoid(h)
        a = (h * s * u).astype(BF)
        a_ref[at] = a
        term = jnp.sum(a.astype(F32) * g, axis=1, keepdims=True)
        ret[i, :, D:] = jnp.broadcast_to(term, (CAP, 128)).astype(BF)
        g = gate * g
        dhu_ref[at, :FF] = (g * u * s * (1.0 + h * (1.0 - s))).astype(BF)
        dhu_ref[at, FF:] = (g * h * s).astype(BF)
        e_ref[at] = (gate * row[:, :D].astype(F32)).astype(BF)
        return carry

    lax.fori_loop(0, N_E, elementwise, 0)

    for m in range(2):
        d2[m] = (
            lax.dot_general(
                rows, dhu_ref[:, m * FF : (m + 1) * FF], ROWS, preferred_element_type=F32
            ).astype(BF).reshape(2 * N_Y, UNIT, FF)
        )
    dd[...] = (
        lax.dot_general(a_ref[...], e_ref[...], ROWS, preferred_element_type=F32)
        .astype(BF).reshape(N_Y, 2, 2, DOWN, D)
    )

    def partial(piece, which, at):
        if piece == 0:
            return d2.at[which, pl.ds(2 * at, 2)]
        return dd.at[at, :, which]

    def paired(piece, at):
        return s2.at[pl.ds(2 * at, 2)] if piece == 0 else sd.at[at]

    given = {}

    def give(piece, offset):
        at = wrap(offset)
        index = offset % N_Y
        given[piece, index] = go(
            partial(piece, other, at), paired(piece, at),
            ssd.at[piece, index], rsd.at[piece, index], sibling,
        )

    for step in range(4):
        for piece in range(2):
            for way in range(2):
                left = STEPS[piece][way] - step
                if left > 0:
                    give(piece, left if way == 0 else -left)
    for piece in range(2):
        give(piece, 0)

    ret[:, :, :D] = (
        lax.dot_general(dhu_ref[:, :FF], w2[0].reshape(D, FF), LAST, preferred_element_type=F32)
        + lax.dot_general(dhu_ref[:, FF:], w2[1].reshape(D, FF), LAST, preferred_element_type=F32)
    ).astype(BF).reshape(N_E, CAP, D)

    def chip_sum(piece, offset):
        given[piece, offset % N_Y].wait_recv()
        at = wrap(offset)
        return partial(piece, core, at)[...].astype(F32) + paired(piece, at)[...].astype(F32)

    out_buf, in_buf = (snd2, sndd), (rec2, recd)
    going = {}

    def reduce_step(piece, way, step):
        left = STEPS[piece][way] - step
        total = chip_sum(piece, left if way == 0 else -left)
        if step > 0:
            going[piece, way].wait_recv()
            total = total + in_buf[piece][way, step - 1].astype(F32)
        out_buf[piece][way, step] = total.astype(BF)
        going[piece, way] = go(
            out_buf[piece].at[way, step], in_buf[piece].at[way, step],
            srs.at[piece, way, step], rrs.at[piece, way, step], ups[way],
        )

    back_rows = []
    for step in range(4):
        for piece in range(2):
            for way in range(2):
                if step < STEPS[piece][way]:
                    reduce_step(piece, way, step)
        if step == 0:
            back_rows = [
                go(ret.at[peer(k)], back.at[ex], sr.at[k], rr.at[k], (dp, peer(k)))
                for k in range(1, N_E)
            ]
            back[ex] = ret[ex]

    kept = []
    crossing = []
    x_out, x_in = (xs2, xsd), (xr2, xrd)
    for piece in range(2):
        total = chip_sum(piece, 0)
        for way in range(2):
            going[piece, way].wait_recv()
            total = total + in_buf[piece][way, STEPS[piece][way] - 1].astype(F32)
        here = xh == 0
        x_out[piece][...] = jnp.where(here, total[1], total[0]).astype(BF)
        kept.append(jnp.where(here, total[0], total[1]))
        crossing.append(
            go(x_out[piece], x_in[piece], sxr.at[piece], rxr.at[piece], partner)
        )

    for piece in range(2):
        crossing[piece].wait_recv()
        kept[piece] = kept[piece] + x_in[piece][...].astype(F32)
    top, bottom = kept[0][:HALF], kept[0][HALF:]
    cs[...] = jnp.where(is_first, bottom, top).astype(BF)
    last = go(cs, cr, scr, rcr, sibling)
    own_half = jnp.where(is_first, top, bottom)
    wd_out[...] = kept[1].astype(BF)

    for copy in back_rows:
        copy.wait_recv()
    place = place_ref[...]
    tok_out[...] = jnp.dot(
        place, back[:, :, :D].reshape(SLOTS, D), preferred_element_type=F32
    ).astype(BF)
    terms = back[:, :, D:].reshape(SLOTS, 128)
    pick = lax.div(lax.broadcasted_iota(jnp.int32, (SLOTS, 128), 0), CAP)
    pick = pick == lax.broadcasted_iota(jnp.int32, (SLOTS, 128), 1)
    terms = jnp.where(pick, terms.astype(F32), 0.0).astype(BF)
    by_expert = jnp.dot(place, terms, preferred_element_type=F32)
    ids = lax.broadcasted_iota(jnp.int32, (TOK, 128), 1) * EXP_DEV
    column = lax.broadcasted_iota(jnp.int32, (TOK, 8), 1)
    result = jnp.zeros((TOK, 8), F32)
    route = routes[...]
    for k in range(8):
        value = jnp.sum(
            jnp.where(route[:, k : k + 1] == ids, by_expert, 0.0), axis=1, keepdims=True
        )
        result = jnp.where(column == k, value, result)
    gate_out[...] = result.astype(BF)

    last.wait_recv()
    arrived = cr[...].astype(F32)
    wg_out[...] = jnp.where(is_first, own_half, arrived).astype(BF)
    wu_out[...] = jnp.where(is_first, arrived, own_half).astype(BF)
    for copy in started:
        copy.wait_send()


def body(tokens, out_grad, routes, gate_values, w_gate, w_up, w_down):
    vmem = pl.BlockSpec(memory_space=pltpu.VMEM)
    dma = pltpu.SemaphoreType.DMA
    shape = jax.ShapeDtypeStruct
    scratch = [
        pltpu.VMEM((TOK, SLOTS), BF),
        pltpu.VMEM((N_E, CAP, D), BF),
        pltpu.VMEM((N_E, CAP, WIDE), BF),
        pltpu.VMEM((N_E, CAP, D), BF),
        pltpu.VMEM((N_E, CAP, WIDE), BF),
        pltpu.VMEM((N_E, CAP, WIDE), BF),
        pltpu.VMEM((N_E, CAP, WIDE), BF),
        pltpu.VMEM((2, HALF, FF), BF),
        pltpu.VMEM((HALF, FF), BF),
        pltpu.VMEM((2, 2 * N_Y, UNIT, FF), BF),
        pltpu.VMEM((N_Y, 2, 2, DOWN, D), BF),
        pltpu.VMEM((SLOTS, FF), F32),
        pltpu.VMEM((SLOTS, FF), F32),
        pltpu.VMEM((SLOTS, FF), F32),
        pltpu.VMEM((SLOTS, FF), BF),
        pltpu.VMEM((SLOTS, 2 * FF), BF),
        pltpu.VMEM((SLOTS, D), BF),
        pltpu.VMEM((2, 2 * N_Y, UNIT, FF), BF),
        pltpu.VMEM((N_Y, 2, 2, DOWN, D), BF),
        pltpu.VMEM((2 * N_Y, UNIT, FF), BF),
        pltpu.VMEM((N_Y, 2, DOWN, D), BF),
        pltpu.VMEM((2, 4, 2, UNIT, FF), BF),
        pltpu.VMEM((2, 4, 2, DOWN, D), BF),
        pltpu.VMEM((2, 4, 2, UNIT, FF), BF),
        pltpu.VMEM((2, 4, 2, DOWN, D), BF),
        pltpu.VMEM((UNIT, FF), BF),
        pltpu.VMEM((DOWN, D), BF),
        pltpu.VMEM((UNIT, FF), BF),
        pltpu.VMEM((DOWN, D), BF),
        pltpu.VMEM((HALF, FF), BF),
        pltpu.VMEM((HALF, FF), BF),
        dma((N_E,)), dma((N_E,)), dma((N_E,)), dma((N_E,)), dma((N_E,)), dma((N_E,)),
        dma, dma,
        dma((2,)), dma((2,)),
        dma((2, 2, 4)), dma((2, 2, 4)),
        dma((2, N_Y)), dma((2, N_Y)),
        dma((2, N_Y)), dma((2, N_Y)),
        dma((2, 2, 4)), dma((2, 2, 4)),
        dma((2,)), dma((2,)),
        dma, dma,
    ]
    outs = pl.pallas_call(
        kernel,
        out_shape=(
            shape((TOK, D), BF), shape((TOK, 8), BF),
            shape((HALF, FF), BF), shape((HALF, FF), BF), shape((DOWN, D), BF),
        ),
        in_specs=[vmem] * 7,
        out_specs=(vmem,) * 5,
        scratch_shapes=scratch,
        compiler_params=pltpu.CompilerParams(
            collective_id=0, has_side_effects=True, vmem_limit_bytes=48 * 1024 * 1024
        ),
    )(tokens, out_grad, routes, gate_values, w_gate[0], w_up[0], w_down[0])
    token_grad, gate_grad, wg, wu, wd = outs
    return token_grad, gate_grad, wg[None], wu[None], wd[None]


def solution(mesh):
    rows = P(("dp", "expert"), None)
    weight = P("expert", "dp", None)
    return jax.shard_map(
        body,
        mesh=mesh,
        in_specs=(rows,) * 4 + (weight,) * 3,
        out_specs=(rows, rows, weight, weight, weight),
        check_vma=False,
    )
```

```python
import jax
import jax.numpy as jnp
from jax import lax
from jax.experimental import pallas as pl
from jax.experimental.pallas import tpu as pltpu
from jax.sharding import PartitionSpec as P

EXP_DEV = 8
MESH = pl.DeviceIdType.MESH
BF = jnp.bfloat16
F32 = jnp.float32
ROWS = (((0,), (0,)), ((), ()))
LAST = (((1,), (1,)), ((), ()))

N_E = 16
N_Y = 8
TOK = 128
CAP = 16
SLOTS = N_E * CAP
D = 1280
FF = 512
WIDE = D + 128
UNIT = 40
DOWN = 16
STEPS = ((4, 3), (3, 4), (4, 3))


def kernel(
    tokens_hbm, grads_hbm, routes_hbm, gates_hbm, wg_hbm, wu_hbm, wd_hbm,
    tok_out, gate_out, wg_out, wu_out, wd_out,
    tokens, grads, routes, gates,
    place_ref, send_x, send_g, send_s, got_x, got_g, got_s, ret, back,
    w_all, wdn, w_mat,
    hu_ref, g_ref, a_ref, dhu_ref, e_ref,
    d2, dd, s2, sd, snd2, sndd, rec2, recd, xq_out, xq_in, xw_out, xw_in,
    loc, ss, rs, sx, rx, sg, rg, sr, rr, sxw, rxw, sxd, rxd, sag, rag, ssw, rsw,
    ssd, rsd, srs, rrs, sxq, rxq, sxr, rxr,
):
    dp = lax.axis_index("dp")
    ex = lax.axis_index("expert")
    core = lax.rem(dp, 2)
    xh = lax.rem(lax.div(dp, 2), 2)
    y = lax.div(dp, 4)
    other = 1 - core
    across = 1 - xh
    low = lax.rem(dp, 4)
    sibling = (dp + 1 - 2 * core, ex)
    partner = (dp + 2 - 4 * xh, ex)
    ups = (
        (lax.rem(y + 1, N_Y) * 4 + low, ex),
        (lax.rem(y + N_Y - 1, N_Y) * 4 + low, ex),
    )

    def wrap(offset):
        return lax.rem(y + (offset + 2 * N_Y), N_Y)

    def peer(k):
        return lax.rem(ex + (k + N_E), N_E)

    started = []

    def go(src, dst, send, recv, to):
        copy = pltpu.make_async_remote_copy(
            src_ref=src, dst_ref=dst, send_sem=send, recv_sem=recv,
            device_id=to, device_id_type=MESH,
        )
        copy.start()
        started.append(copy)
        return copy

    barrier = pltpu.get_barrier_semaphore()
    for to in (sibling, partner) + ups:
        pl.semaphore_signal(barrier, inc=1, device_id=to, device_id_type=MESH)
    for k in range(1, N_E):
        pl.semaphore_signal(barrier, inc=1, device_id=(dp, peer(k)), device_id_type=MESH)

    local = []
    for i, (src, dst) in enumerate((
        (routes_hbm, routes), (gates_hbm, gates), (tokens_hbm, tokens),
        (wg_hbm.at[0], w_all.at[y, xh, core, :, pl.ds(0, FF)]),
        (wu_hbm.at[0], w_all.at[y, xh, core, :, pl.ds(FF, FF)]),
        (wd_hbm.at[0], wdn.at[y, xh, core]), (grads_hbm, grads),
    )):
        local.append(pltpu.make_async_copy(src, dst, loc.at[i]))
        local[-1].start()

    line = lax.broadcasted_iota(jnp.int32, (SLOTS, TOK), 0)
    expert_id = lax.div(line, CAP) * EXP_DEV
    slot_id = lax.rem(line, CAP)
    before = (
        lax.broadcasted_iota(jnp.int32, (TOK, TOK), 0)
        < lax.broadcasted_iota(jnp.int32, (TOK, TOK), 1)
    )
    before = jnp.where(before, 1.0, 0.0).astype(BF)
    local[0].wait()
    local[1].wait()
    route = routes[...]
    gate_wide = gates[...].astype(F32)
    chosen = jnp.zeros((SLOTS, TOK), F32)
    gate_tok = jnp.zeros((SLOTS, TOK), F32)
    for k in range(8):
        match = route[k : k + 1] == expert_id
        chosen = jnp.where(match, 1.0, chosen)
        gate_tok = jnp.where(match, gate_wide[k : k + 1], gate_tok)
    rank = jnp.dot(chosen.astype(BF), before, preferred_element_type=F32)
    placing = jnp.where(rank == slot_id.astype(F32), chosen, 0.0)
    gate_column = jnp.sum(placing * gate_tok, axis=1, keepdims=True)
    placing = placing.astype(BF)
    place_ref[...] = placing
    local[2].wait()
    send_x[...] = (
        jnp.dot(placing, tokens[...], preferred_element_type=F32)
        .astype(BF).reshape(N_E, CAP, D)
    )
    gate_rows = jnp.broadcast_to(gate_column, (SLOTS, 128)).reshape(N_E, CAP, 128)
    diagonal = (
        lax.broadcasted_iota(jnp.int32, (CAP, 128), 0)
        == lax.broadcasted_iota(jnp.int32, (CAP, 128), 1)
    )
    send_s[...] = jnp.sum(jnp.where(diagonal[None], gate_rows, 0.0), axis=1, keepdims=True)
    for i in range(3, 6):
        local[i].wait()

    pl.semaphore_wait(barrier, 4 + N_E - 1)

    def block(piece, at):
        if piece < 2:
            return w_all.at[at, xh if piece == 0 else across, core]
        return wdn.at[at, xh if piece == 2 else across, core]

    def ring_send(piece, way, step):
        at = block(piece, wrap(-step if way == 0 else step))
        return go(at, at, sag.at[piece, way, step], rag.at[piece, way, step], ups[way])

    shared = []

    def to_sibling(piece, offset, index):
        at = block(piece, wrap(offset))
        shared.append(go(at, at, ssw.at[piece, index], rsw.at[piece, index], sibling))

    def to_partner(offset, index):
        at = block(2, wrap(offset))
        return go(at, at, sxd.at[index], rxd.at[index], partner)

    ring = {}
    crossed = {}
    for way in range(2):
        ring[0, way] = ring_send(0, way, 0)
    mine = block(0, y)
    part = go(mine, mine, sxw, rxw, partner)
    for way in range(2):
        ring[2, way] = ring_send(2, way, 0)
    row_x = [
        go(send_x.at[peer(k)], got_x.at[ex], sx.at[k], rx.at[k], (dp, peer(k)))
        for k in range(1, N_E)
    ]
    crossed[0] = to_partner(0, 0)
    to_sibling(0, 0, 0)
    to_sibling(2, 0, 0)
    got_x[ex] = send_x[ex]
    row_s = [
        go(send_s.at[peer(k)], got_s.at[ex], ss.at[k], rs.at[k], (dp, peer(k)))
        for k in range(1, N_E)
    ]
    got_s[ex] = send_s[ex]

    local[6].wait()
    send_g[...] = (
        jnp.dot(placing, grads[...], preferred_element_type=F32)
        .astype(BF).reshape(N_E, CAP, D)
    )
    got_g[ex] = send_g[ex]

    part.wait_recv()
    for way in range(2):
        ring[1, way] = ring_send(1, way, 0)
    row_g = [
        go(send_g.at[peer(k)], got_g.at[ex], sg.at[k], rg.at[k], (dp, peer(k)))
        for k in range(1, N_E)
    ]
    to_sibling(1, 0, 0)

    late = [(0, 0)]
    for step in range(4):
        fresh = []
        for piece in range(3):
            for way in range(2):
                if step < STEPS[piece][way]:
                    ring[piece, way].wait_recv()
                    if step + 1 < STEPS[piece][way]:
                        ring[piece, way] = ring_send(piece, way, step + 1)
                    offset = -1 - step if way == 0 else 1 + step
                    index = 1 + step if way == 0 else 1 + STEPS[piece][0] + step
                    if piece == 2:
                        crossed[index] = to_partner(offset, index)
                        fresh.append((offset, index))
                    to_sibling(piece, offset, index)
        for offset, index in late:
            crossed[index].wait_recv()
            to_sibling(3, offset, index)
        late = fresh
    for offset, index in late:
        crossed[index].wait_recv()
        to_sibling(3, offset, index)
    for copy in shared:
        copy.wait_recv()

    def flatten(i, carry):
        at = pl.ds(pl.multiple_of(i * 4 * UNIT, 4 * UNIT), 4 * UNIT)
        w_mat[at] = w_all[i].astype(F32).reshape(4 * UNIT, 2 * FF).astype(BF)
        return carry

    lax.fori_loop(0, N_Y, flatten, 0)
    for copy in row_x:
        copy.wait_recv()
    rows = got_x[...].reshape(SLOTS, D)
    hu_ref[...] = jnp.dot(rows, w_mat[...], preferred_element_type=F32)
    for copy in row_s:
        copy.wait_recv()
    for copy in row_g:
        copy.wait_recv()
    g_ref[...] = lax.dot_general(
        got_g[...].reshape(SLOTS, D), wdn[...].reshape(FF, D), LAST,
        preferred_element_type=F32,
    )

    def elementwise(i, carry):
        at = pl.ds(pl.multiple_of(i * CAP, CAP), CAP)
        h, u, g = hu_ref[at, :FF], hu_ref[at, FF:], g_ref[at]
        gate = jnp.sum(
            jnp.where(diagonal, jnp.broadcast_to(got_s[i], (CAP, 128)), 0.0),
            axis=1, keepdims=True,
        )
        s = jax.nn.sigmoid(h)
        a = (h * s * u).astype(BF)
        a_ref[at] = a
        term = jnp.sum(a.astype(F32) * g, axis=1, keepdims=True)
        ret[i, :, D:] = jnp.broadcast_to(term, (CAP, 128)).astype(BF)
        g = gate * g
        dhu_ref[at, :FF] = (g * u * s * (1.0 + h * (1.0 - s))).astype(BF)
        dhu_ref[at, FF:] = (g * h * s).astype(BF)
        e_ref[at] = (gate * got_g[i].astype(F32)).astype(BF)
        return carry

    lax.fori_loop(0, N_E, elementwise, 0)

    given = {}
    partial, paired = (d2, dd), (s2, sd)

    def give(kind, offset):
        at = wrap(offset)
        index = offset % N_Y
        given[kind, index] = go(
            partial[kind].at[at, :, other], paired[kind].at[at],
            ssd.at[kind, index], rsd.at[kind, index], sibling,
        )

    order = (4, -3, 3, 2, -2, 1, -1, 0)
    d2[...] = (
        lax.dot_general(rows, dhu_ref[...], ROWS, preferred_element_type=F32)
        .reshape(N_Y, 2, 2, UNIT, 2 * FF).astype(BF)
    )
    for offset in order:
        give(0, offset)
    dd[...] = (
        lax.dot_general(a_ref[...], e_ref[...], ROWS, preferred_element_type=F32)
        .astype(BF).reshape(N_Y, 2, 2, DOWN, D)
    )
    for offset in order:
        give(1, offset)

    arrived = set()

    def chip_sum(kind, offset, half):
        index = offset % N_Y
        if (kind, index) not in arrived:
            arrived.add((kind, index))
            given[kind, index].wait_recv()
        at = wrap(offset)
        return partial[kind][at, half, core].astype(F32) + paired[kind][at, half].astype(F32)

    def send_buf(piece, way, step):
        return snd2.at[piece, way, step] if piece < 2 else sndd.at[way, step]

    def recv_buf(piece, way, step):
        return rec2.at[piece, way, step] if piece < 2 else recd.at[way, step]

    going = {}
    swapped = {}

    def own_term(piece, offset):
        if piece == 0:
            return chip_sum(0, offset, across)
        if piece == 1:
            return chip_sum(0, offset, xh)
        swapped[offset % N_Y].wait_recv()
        return chip_sum(1, offset, xh) + xq_in[offset % N_Y].astype(F32)

    def reduce_step(piece, way, step):
        left = STEPS[piece][way] - step
        total = own_term(piece, left if way == 0 else -left)
        if step > 0:
            going[piece, way].wait_recv()
            total = total + recv_buf(piece, way, step - 1)[...].astype(F32)
        src = send_buf(piece, way, step)
        src[...] = total.astype(BF)
        going[piece, way] = go(
            src, recv_buf(piece, way, step),
            srs.at[piece, way, step], rrs.at[piece, way, step], ups[way],
        )

    for piece in range(2):
        for way in range(2):
            reduce_step(piece, way, 0)
    for offset in order:
        index = offset % N_Y
        xq_out[index] = chip_sum(1, offset, across).astype(BF)
        swapped[index] = go(
            xq_out.at[index], xq_in.at[index], sxq.at[index], rxq.at[index], partner
        )
    ret[:, :, :D] = (
        lax.dot_general(dhu_ref[...], w_mat[...], LAST, preferred_element_type=F32)
        .astype(BF).reshape(N_E, CAP, D)
    )
    back_rows = [
        go(ret.at[peer(k)], back.at[ex], sr.at[k], rr.at[k], (dp, peer(k)))
        for k in range(1, N_E)
    ]
    back[ex] = ret[ex]
    for step in range(1, 5):
        for piece in range(2):
            for way in range(2):
                if step < STEPS[piece][way]:
                    reduce_step(piece, way, step)
        for way in range(2):
            if step - 1 < STEPS[2][way]:
                reduce_step(2, way, step - 1)

    def ring_total(piece):
        total = own_term(piece, 0)
        for way in range(2):
            going[piece, way].wait_recv()
            total = total + recv_buf(piece, way, STEPS[piece][way] - 1)[...].astype(F32)
        return total

    xw_out[...] = ring_total(0).astype(BF)
    crossing = go(xw_out, xw_in, sxr, rxr, partner)
    kept = ring_total(1)
    wd_out[...] = ring_total(2).astype(BF)

    for copy in back_rows:
        copy.wait_recv()
    place = place_ref[...]
    tok_out[...] = lax.dot_general(
        place, back[:, :, :D].reshape(SLOTS, D), ROWS, preferred_element_type=F32
    ).astype(BF)
    terms = back[:, :, D:].reshape(SLOTS, 128)
    pick = lax.div(lax.broadcasted_iota(jnp.int32, (SLOTS, 128), 0), CAP)
    pick = pick == lax.broadcasted_iota(jnp.int32, (SLOTS, 128), 1)
    terms = jnp.where(pick, terms.astype(F32), 0.0).astype(BF)
    by_expert = lax.dot_general(terms, place, ROWS, preferred_element_type=F32)[:N_E]
    ids = lax.broadcasted_iota(jnp.int32, (N_E, TOK), 0) * EXP_DEV
    line = lax.broadcasted_iota(jnp.int32, (8, TOK), 0)
    result = jnp.zeros((8, TOK), F32)
    route = routes[...]
    for k in range(8):
        value = jnp.sum(
            jnp.where(route[k : k + 1] == ids, by_expert, 0.0), axis=0, keepdims=True
        )
        result = jnp.where(line == k, value, result)
    gate_out[...] = result.astype(BF)

    crossing.wait_recv()
    kept = (kept + xw_in[...].astype(F32)).astype(BF)
    wg_out[...] = kept[:, :FF]
    wu_out[...] = kept[:, FF:]
    for copy in started:
        copy.wait_send()


def body(tokens, out_grad, routes, gate_values, w_gate, w_up, w_down):
    anywhere = pl.BlockSpec(memory_space=pl.ANY)
    vmem = pl.BlockSpec(memory_space=pltpu.VMEM)
    dma = pltpu.SemaphoreType.DMA
    shape = jax.ShapeDtypeStruct
    scratch = [
        pltpu.VMEM((TOK, D), BF),
        pltpu.VMEM((TOK, D), BF),
        pltpu.VMEM((8, TOK), jnp.int32),
        pltpu.VMEM((8, TOK), BF),
        pltpu.VMEM((SLOTS, TOK), BF),
        pltpu.VMEM((N_E, CAP, D), BF),
        pltpu.VMEM((N_E, CAP, D), BF),
        pltpu.VMEM((N_E, 1, 128), F32),
        pltpu.VMEM((N_E, CAP, D), BF),
        pltpu.VMEM((N_E, CAP, D), BF),
        pltpu.VMEM((N_E, 1, 128), F32),
        pltpu.VMEM((N_E, CAP, WIDE), BF),
        pltpu.VMEM((N_E, CAP, WIDE), BF),
        pltpu.VMEM((N_Y, 2, 2, UNIT, 2 * FF), BF),
        pltpu.VMEM((N_Y, 2, 2, DOWN, D), BF),
        pltpu.VMEM((D, 2 * FF), BF),
        pltpu.VMEM((SLOTS, 2 * FF), F32),
        pltpu.VMEM((SLOTS, FF), F32),
        pltpu.VMEM((SLOTS, FF), BF),
        pltpu.VMEM((SLOTS, 2 * FF), BF),
        pltpu.VMEM((SLOTS, D), BF),
        pltpu.VMEM((N_Y, 2, 2, UNIT, 2 * FF), BF),
        pltpu.VMEM((N_Y, 2, 2, DOWN, D), BF),
        pltpu.VMEM((N_Y, 2, UNIT, 2 * FF), BF),
        pltpu.VMEM((N_Y, 2, DOWN, D), BF),
        pltpu.VMEM((2, 2, 4, UNIT, 2 * FF), BF),
        pltpu.VMEM((2, 4, DOWN, D), BF),
        pltpu.VMEM((2, 2, 4, UNIT, 2 * FF), BF),
        pltpu.VMEM((2, 4, DOWN, D), BF),
        pltpu.VMEM((N_Y, DOWN, D), BF),
        pltpu.VMEM((N_Y, DOWN, D), BF),
        pltpu.VMEM((UNIT, 2 * FF), BF),
        pltpu.VMEM((UNIT, 2 * FF), BF),
        dma((7,)),
        dma((N_E,)), dma((N_E,)), dma((N_E,)), dma((N_E,)),
        dma((N_E,)), dma((N_E,)), dma((N_E,)), dma((N_E,)),
        dma, dma,
        dma((N_Y,)), dma((N_Y,)),
        dma((3, 2, 4)), dma((3, 2, 4)),
        dma((4, N_Y)), dma((4, N_Y)),
        dma((2, N_Y)), dma((2, N_Y)),
        dma((3, 2, 4)), dma((3, 2, 4)),
        dma((N_Y,)), dma((N_Y,)),
        dma, dma,
    ]
    return pl.pallas_call(
        kernel,
        out_shape=(
            shape((TOK, D), BF), shape((8, TOK), BF),
            shape((UNIT, FF), BF), shape((UNIT, FF), BF), shape((DOWN, D), BF),
        ),
        in_specs=[anywhere] * 7,
        out_specs=(vmem,) * 5,
        scratch_shapes=scratch,
        compiler_params=pltpu.CompilerParams(
            collective_id=0, has_side_effects=True, vmem_limit_bytes=60 * 1024 * 1024
        ),
    )(tokens, out_grad, routes.T, gate_values.T, w_gate, w_up, w_down)


def solution(mesh):
    rows = P(("dp", "expert"), None)
    weight = P("expert", "dp", None)

    def whole(*args):
        token_grad, gate_grad, wg, wu, wd = body(*args)
        return token_grad, gate_grad.T, wg[None], wu[None], wd[None]

    return jax.shard_map(
        whole,
        mesh=mesh,
        in_specs=(rows,) * 4 + (weight,) * 3,
        out_specs=(rows, rows, weight, weight, weight),
        check_vma=False,
    )
```

```python
import jax
import jax.numpy as jnp
from jax import lax
from jax.experimental import pallas as pl
from jax.experimental.pallas import tpu as pltpu
from jax.sharding import PartitionSpec as P

EXP_DEV = 8
MESH = pl.DeviceIdType.MESH
BF = jnp.bfloat16
F32 = jnp.float32
ROWS = (((0,), (0,)), ((), ()))
LAST = (((1,), (1,)), ((), ()))

N_E = 16
N_Y = 8
TOK = 128
CAP = 16
SLOTS = N_E * CAP
D = 1280
FF = 512
WIDE = D + 128
UNIT = 40
DOWN = 16
PEERS = (8, 7, 9, 6, 10, 5, 11, 4, 12, 3, 13, 2, 14, 1, 15)
STEPS = ((4, 3), (3, 4), (4, 3))
PARTS = ((4, 3), (4, 3), (3, 4), (3, 4), (3, 4))
LAST_IN = 3


def kernel(
    tokens_hbm, grads_hbm, routes_hbm, gates_hbm, wg_hbm, wu_hbm, wd_hbm,
    tok_hbm, gate_hbm, wg_out_hbm, wu_out_hbm, wd_out_hbm,
    tok_out, gate_out, wg_out, wu_out, wd_out,
    tokens, grads, routes, gates,
    place_ref, send_x, send_g, send_s, got_x, got_g, got_s, ret, back,
    w_all, wdn, w_mat, xt_ref, wdt_ref,
    hu_ref, g_ref, a_ref, dhu_ref, e_ref,
    d2, dd, s2, sd, snd2, sndd, rec2, recd, xq_out, xq_in, xw_out, xw_in,
    loc, ss, rs, sx, rx, sg, rg, sr, rr, sxw, rxw, sxd, rxd, sag, rag, ssw, rsw,
    ssd, rsd, srs, rrs, sxq, rxq, sxr, rxr,
):
    dp = lax.axis_index("dp")
    ex = lax.axis_index("expert")
    core = lax.rem(dp, 2)
    xh = lax.rem(lax.div(dp, 2), 2)
    y = lax.div(dp, 4)
    other = 1 - core
    across = 1 - xh
    low = lax.rem(dp, 4)
    sibling = (dp + 1 - 2 * core, ex)
    partner = (dp + 2 - 4 * xh, ex)
    ups = (
        (lax.rem(y + 1, N_Y) * 4 + low, ex),
        (lax.rem(y + N_Y - 1, N_Y) * 4 + low, ex),
    )

    def wrap(offset):
        return lax.rem(y + (offset + 2 * N_Y), N_Y)

    def peer(k):
        return lax.rem(ex + (k + N_E), N_E)

    started = []

    def go(src, dst, send, recv, to):
        copy = pltpu.make_async_remote_copy(
            src_ref=src, dst_ref=dst, send_sem=send, recv_sem=recv,
            device_id=to, device_id_type=MESH,
        )
        copy.start()
        started.append(copy)
        return copy

    leaving = []

    def leave(i, src, dst):
        leaving.append(pltpu.make_async_copy(src, dst, loc.at[7 + i]))
        leaving[-1].start()

    barrier = pltpu.get_barrier_semaphore()
    for to in (sibling, partner) + ups:
        pl.semaphore_signal(barrier, inc=1, device_id=to, device_id_type=MESH)
    for k in range(1, N_E):
        pl.semaphore_signal(barrier, inc=1, device_id=(dp, peer(k)), device_id_type=MESH)

    local = []
    for i, (src, dst) in enumerate((
        (routes_hbm, routes), (gates_hbm, gates), (tokens_hbm, tokens),
        (wg_hbm.at[0], w_all.at[y, xh, core, :, pl.ds(0, FF)]),
        (wu_hbm.at[0], w_all.at[y, xh, core, :, pl.ds(FF, FF)]),
        (wd_hbm.at[0], wdn.at[y, xh, core]), (grads_hbm, grads),
    )):
        local.append(pltpu.make_async_copy(src, dst, loc.at[i]))
        local[-1].start()

    line = lax.broadcasted_iota(jnp.int32, (SLOTS, TOK), 0)
    expert_id = lax.div(line, CAP) * EXP_DEV
    slot_id = lax.rem(line, CAP)
    before = (
        lax.broadcasted_iota(jnp.int32, (TOK, TOK), 0)
        < lax.broadcasted_iota(jnp.int32, (TOK, TOK), 1)
    )
    before = jnp.where(before, 1.0, 0.0).astype(BF)
    local[0].wait()
    route = routes[...]
    chosen = jnp.zeros((SLOTS, TOK), F32)
    for k in range(8):
        match = route[k : k + 1] == expert_id
        chosen = jnp.where(match, 1.0, chosen)
    rank = jnp.dot(chosen.astype(BF), before, preferred_element_type=F32)
    placing = jnp.where(rank == slot_id.astype(F32), chosen, 0.0)
    placing = placing.astype(BF)
    local[2].wait()
    send_x[...] = (
        jnp.dot(placing, tokens[...], preferred_element_type=F32)
        .astype(BF).reshape(N_E, CAP, D)
    )

    pl.semaphore_wait(barrier, 4 + N_E - 1)

    row_x = [
        go(send_x.at[peer(k)], got_x.at[ex], sx.at[k], rx.at[k], (dp, peer(k)))
        for k in PEERS
    ]
    for i in range(3, 6):
        local[i].wait()

    def block(piece, at):
        if piece < 2:
            return w_all.at[at, xh if piece == 0 else across, core]
        return wdn.at[at, xh if piece == 2 else across, core]

    def ring_send(piece, way, step):
        at = block(piece, wrap(-step if way == 0 else step))
        return go(at, at, sag.at[piece, way, step], rag.at[piece, way, step], ups[way])

    shared = []

    def to_sibling(piece, offset, index):
        at = block(piece, wrap(offset))
        shared.append(go(at, at, ssw.at[piece, index], rsw.at[piece, index], sibling))

    def to_partner(offset, index):
        at = block(2, wrap(offset))
        return go(at, at, sxd.at[index], rxd.at[index], partner)

    ring = {}
    crossed = {}
    for way in range(2):
        ring[0, way] = ring_send(0, way, 0)
    mine = block(0, y)
    part = go(mine, mine, sxw, rxw, partner)
    for way in range(2):
        ring[2, way] = ring_send(2, way, 0)
    crossed[0] = to_partner(0, 0)
    to_sibling(0, 0, 0)
    to_sibling(2, 0, 0)
    got_x[ex] = send_x[ex]
    place_ref[...] = placing
    local[1].wait()
    gate_wide = gates[...].astype(F32)
    gate_tok = jnp.zeros((SLOTS, TOK), F32)
    for k in range(8):
        gate_tok = jnp.where(route[k : k + 1] == expert_id, gate_wide[k : k + 1], gate_tok)
    gate_column = jnp.sum(placing.astype(F32) * gate_tok, axis=1, keepdims=True)
    gate_rows = jnp.broadcast_to(gate_column, (SLOTS, 128)).reshape(N_E, CAP, 128)
    diagonal = (
        lax.broadcasted_iota(jnp.int32, (CAP, 128), 0)
        == lax.broadcasted_iota(jnp.int32, (CAP, 128), 1)
    )
    send_s[...] = jnp.sum(jnp.where(diagonal[None], gate_rows, 0.0), axis=1, keepdims=True)
    row_s = [
        go(send_s.at[peer(k)], got_s.at[ex], ss.at[k], rs.at[k], (dp, peer(k)))
        for k in PEERS
    ]
    got_s[ex] = send_s[ex]

    local[6].wait()
    send_g[...] = (
        jnp.dot(placing, grads[...], preferred_element_type=F32)
        .astype(BF).reshape(N_E, CAP, D)
    )
    got_g[ex] = send_g[ex]

    part.wait_recv()
    for way in range(2):
        ring[1, way] = ring_send(1, way, 0)
    row_g = [
        go(send_g.at[peer(k)], got_g.at[ex], sg.at[k], rg.at[k], (dp, peer(k)))
        for k in PEERS
    ]
    to_sibling(1, 0, 0)

    late = [(0, 0)]
    for step in range(4):
        fresh = []
        for piece in range(3):
            for way in range(2):
                if step < STEPS[piece][way]:
                    ring[piece, way].wait_recv()
                    if step + 1 < STEPS[piece][way]:
                        ring[piece, way] = ring_send(piece, way, step + 1)
                    offset = -1 - step if way == 0 else 1 + step
                    index = 1 + step if way == 0 else 1 + STEPS[piece][0] + step
                    if piece == 2:
                        crossed[index] = to_partner(offset, index)
                        fresh.append((offset, index))
                    to_sibling(piece, offset, index)
        for offset, index in late:
            crossed[index].wait_recv()
            to_sibling(3, offset, index)
        late = fresh
    for offset, index in late:
        crossed[index].wait_recv()
        to_sibling(3, offset, index)
    for copy in shared:
        copy.wait_recv()

    def flatten(i, carry):
        at = pl.ds(pl.multiple_of(i * 4 * UNIT, 4 * UNIT), 4 * UNIT)
        w_mat[at] = w_all[i].astype(F32).reshape(4 * UNIT, 2 * FF).astype(BF)
        return carry

    lax.fori_loop(0, N_Y, flatten, 0)
    for copy in row_x:
        copy.wait_recv()
    rows = got_x[...].reshape(SLOTS, D)
    hu_ref[...] = jnp.dot(rows, w_mat[...], preferred_element_type=F32)
    xt_ref[...] = rows.T
    wdt_ref[...] = wdn[...].reshape(FF, D).T
    for copy in row_s:
        copy.wait_recv()

    def act_grad(sources):
        got = jnp.concatenate([got_g[i] for i in sources], axis=0)
        g = jnp.dot(got, wdt_ref[...], preferred_element_type=F32)
        for n, i in enumerate(sources):
            g_ref[pl.ds(pl.multiple_of(i * CAP, CAP), CAP)] = g[n * CAP : (n + 1) * CAP]

    def elementwise(i):
        at = pl.ds(pl.multiple_of(i * CAP, CAP), CAP)
        h, u, g = hu_ref[at, :FF], hu_ref[at, FF:], g_ref[at]
        gate = jnp.sum(
            jnp.where(diagonal, jnp.broadcast_to(got_s[i], (CAP, 128)), 0.0),
            axis=1, keepdims=True,
        )
        s = jax.nn.sigmoid(h)
        a = (h * s * u).astype(BF)
        a_ref[at] = a
        term = jnp.sum(a.astype(F32) * g, axis=1, keepdims=True)
        ret[i, :, D:] = jnp.broadcast_to(term, (CAP, 128)).astype(BF)
        g = gate * g
        dhu_ref[at, :FF] = (g * u * s * (1.0 + h * (1.0 - s))).astype(BF)
        dhu_ref[at, FF:] = (g * h * s).astype(BF)
        e_ref[at] = (gate * got_g[i].astype(F32)).astype(BF)

    def turn(n, carry):
        k = 8 + lax.div(n + 1, 2) * (1 - 2 * lax.rem(n, 2))
        elementwise(lax.rem(ex + N_E - k, N_E))
        return carry

    early = N_E - 1 - LAST_IN
    for copy in row_g[:early]:
        copy.wait_recv()
    act_grad([ex] + [peer(-k) for k in PEERS[:early]])
    elementwise(ex)
    lax.fori_loop(0, early, turn, 0)
    for copy in row_g[early:]:
        copy.wait_recv()
    act_grad([peer(-k) for k in PEERS[early:]])
    lax.fori_loop(early, N_E - 1, turn, 0)

    given = {}
    partial, paired = (d2, dd), (s2, sd)

    def give(kind, offset):
        at = wrap(offset)
        index = offset % N_Y
        given[kind, index] = go(
            partial[kind].at[at, :, other], paired[kind].at[at],
            ssd.at[kind, index], rsd.at[kind, index], sibling,
        )

    order = (4, -3, 3, 2, -2, 1, -1, 0)
    dd[...] = (
        lax.dot_general(a_ref[...], e_ref[...], ROWS, preferred_element_type=F32)
        .astype(BF).reshape(N_Y, 2, 2, DOWN, D)
    )
    for offset in order:
        give(1, offset)
    for offset in order:
        at = wrap(offset)
        d2[at] = (
            jnp.dot(
                xt_ref[pl.ds(pl.multiple_of(at * 4 * UNIT, 4 * UNIT), 4 * UNIT)], dhu_ref[...],
                preferred_element_type=F32,
            ).reshape(2, 2, UNIT, 2 * FF).astype(BF)
        )
        give(0, offset)

    arrived = set()

    def chip_sum(kind, offset, half, lanes=slice(None)):
        index = offset % N_Y
        if (kind, index) not in arrived:
            arrived.add((kind, index))
            given[kind, index].wait_recv()
        at = wrap(offset)
        own, came = partial[kind], paired[kind]
        return own[at, half, core, :, lanes].astype(F32) + came[at, half, :, lanes].astype(F32)

    def send_buf(piece, way, step):
        return snd2.at[piece, way, step] if piece < 4 else sndd.at[way, step]

    def recv_buf(piece, way, step):
        return rec2.at[piece, way, step] if piece < 4 else recd.at[way, step]

    going = {}
    swapped = {}

    def own_term(piece, offset):
        if piece < 4:
            lanes = slice(0, FF) if piece % 2 == 0 else slice(FF, 2 * FF)
            return chip_sum(0, offset, across if piece < 2 else xh, lanes)
        swapped[offset % N_Y].wait_recv()
        return chip_sum(1, offset, xh) + xq_in[offset % N_Y].astype(F32)

    def reduce_step(piece, way, step):
        left = PARTS[piece][way] - step
        total = own_term(piece, left if way == 0 else -left)
        if step > 0:
            going[piece, way].wait_recv()
            total = total + recv_buf(piece, way, step - 1)[...].astype(F32)
        src = send_buf(piece, way, step)
        src[...] = total.astype(BF)
        going[piece, way] = go(
            src, recv_buf(piece, way, step),
            srs.at[piece, way, step], rrs.at[piece, way, step], ups[way],
        )

    for piece in range(2):
        for way in range(2):
            reduce_step(piece, way, 0)
    for offset in (3, -4, 2, -3, 1, -2, -1, 0):
        index = offset % N_Y
        xq_out[index] = chip_sum(1, offset, across).astype(BF)
        swapped[index] = go(
            xq_out.at[index], xq_in.at[index], sxq.at[index], rxq.at[index], partner
        )
    for piece in range(2, 4):
        for way in range(2):
            reduce_step(piece, way, 0)
    ret[:, :, :D] = (
        lax.dot_general(dhu_ref[...], w_mat[...], LAST, preferred_element_type=F32)
        .astype(BF).reshape(N_E, CAP, D)
    )
    back_rows = [
        go(ret.at[peer(k)], back.at[ex], sr.at[k], rr.at[k], (dp, peer(k)))
        for k in PEERS
    ]
    back[ex] = ret[ex]
    for step in range(4):
        for piece in range(4):
            for way in range(2):
                if 0 < step < PARTS[piece][way]:
                    reduce_step(piece, way, step)
        for way in range(2):
            if step < PARTS[4][way]:
                reduce_step(4, way, step)

    def ring_total(piece):
        total = own_term(piece, 0)
        for way in range(2):
            going[piece, way].wait_recv()
            total = total + recv_buf(piece, way, PARTS[piece][way] - 1)[...].astype(F32)
        return total

    crossing = []
    for piece in range(2):
        xw_out[piece] = ring_total(piece).astype(BF)
        crossing.append(
            go(xw_out.at[piece], xw_in.at[piece], sxr.at[piece], rxr.at[piece], partner)
        )
    kept = [ring_total(2), ring_total(3)]
    wd_out[...] = ring_total(4).astype(BF)
    leave(4, wd_out, wd_out_hbm)

    for copy in back_rows:
        copy.wait_recv()
    place = place_ref[...]
    tok_out[...] = lax.dot_general(
        place, back[:, :, :D].reshape(SLOTS, D), ROWS, preferred_element_type=F32
    ).astype(BF)
    leave(0, tok_out, tok_hbm)
    terms = back[:, :, D:].reshape(SLOTS, 128)
    pick = lax.div(lax.broadcasted_iota(jnp.int32, (SLOTS, 128), 0), CAP)
    pick = pick == lax.broadcasted_iota(jnp.int32, (SLOTS, 128), 1)
    terms = jnp.where(pick, terms.astype(F32), 0.0).astype(BF)
    by_expert = lax.dot_general(terms, place, ROWS, preferred_element_type=F32)[:N_E]
    ids = lax.broadcasted_iota(jnp.int32, (N_E, TOK), 0) * EXP_DEV
    line = lax.broadcasted_iota(jnp.int32, (8, TOK), 0)
    result = jnp.zeros((8, TOK), F32)
    route = routes[...]
    for k in range(8):
        value = jnp.sum(
            jnp.where(route[k : k + 1] == ids, by_expert, 0.0), axis=0, keepdims=True
        )
        result = jnp.where(line == k, value, result)
    gate_out[...] = result.astype(BF)
    leave(1, gate_out, gate_hbm)

    for piece, out in enumerate((wg_out, wu_out)):
        crossing[piece].wait_recv()
        out[...] = (kept[piece] + xw_in[piece].astype(F32)).astype(BF)
    leave(2, wg_out, wg_out_hbm)
    leave(3, wu_out, wu_out_hbm)
    for copy in leaving:
        copy.wait()
    for copy in started:
        copy.wait_send()


def hand_over(*refs):
    for i in range(5):
        refs[5 + i][...] = refs[i][...].reshape(refs[5 + i].shape)


def body(tokens, out_grad, routes, gate_values, w_gate, w_up, w_down):
    anywhere = pl.BlockSpec(memory_space=pl.ANY)
    vmem = pl.BlockSpec(memory_space=pltpu.VMEM)
    dma = pltpu.SemaphoreType.DMA
    shape = jax.ShapeDtypeStruct
    scratch = [
        pltpu.VMEM((TOK, D), BF),
        pltpu.VMEM((8, TOK), BF),
        pltpu.VMEM((UNIT, FF), BF),
        pltpu.VMEM((UNIT, FF), BF),
        pltpu.VMEM((DOWN, D), BF),
        pltpu.VMEM((TOK, D), BF),
        pltpu.VMEM((TOK, D), BF),
        pltpu.VMEM((8, TOK), jnp.int32),
        pltpu.VMEM((8, TOK), BF),
        pltpu.VMEM((SLOTS, TOK), BF),
        pltpu.VMEM((N_E, CAP, D), BF),
        pltpu.VMEM((N_E, CAP, D), BF),
        pltpu.VMEM((N_E, 1, 128), F32),
        pltpu.VMEM((N_E, CAP, D), BF),
        pltpu.VMEM((N_E, CAP, D), BF),
        pltpu.VMEM((N_E, 1, 128), F32),
        pltpu.VMEM((N_E, CAP, WIDE), BF),
        pltpu.VMEM((N_E, CAP, WIDE), BF),
        pltpu.VMEM((N_Y, 2, 2, UNIT, 2 * FF), BF),
        pltpu.VMEM((N_Y, 2, 2, DOWN, D), BF),
        pltpu.VMEM((D, 2 * FF), BF),
        pltpu.VMEM((D, SLOTS), BF),
        pltpu.VMEM((D, FF), BF),
        pltpu.VMEM((SLOTS, 2 * FF), F32),
        pltpu.VMEM((SLOTS, FF), F32),
        pltpu.VMEM((SLOTS, FF), BF),
        pltpu.VMEM((SLOTS, 2 * FF), BF),
        pltpu.VMEM((SLOTS, D), BF),
        pltpu.VMEM((N_Y, 2, 2, UNIT, 2 * FF), BF),
        pltpu.VMEM((N_Y, 2, 2, DOWN, D), BF),
        pltpu.VMEM((N_Y, 2, UNIT, 2 * FF), BF),
        pltpu.VMEM((N_Y, 2, DOWN, D), BF),
        pltpu.VMEM((4, 2, 4, UNIT, FF), BF),
        pltpu.VMEM((2, 4, DOWN, D), BF),
        pltpu.VMEM((4, 2, 4, UNIT, FF), BF),
        pltpu.VMEM((2, 4, DOWN, D), BF),
        pltpu.VMEM((N_Y, DOWN, D), BF),
        pltpu.VMEM((N_Y, DOWN, D), BF),
        pltpu.VMEM((2, UNIT, FF), BF),
        pltpu.VMEM((2, UNIT, FF), BF),
        dma((12,)),
        dma((N_E,)), dma((N_E,)), dma((N_E,)), dma((N_E,)),
        dma((N_E,)), dma((N_E,)), dma((N_E,)), dma((N_E,)),
        dma, dma,
        dma((N_Y,)), dma((N_Y,)),
        dma((3, 2, 4)), dma((3, 2, 4)),
        dma((4, N_Y)), dma((4, N_Y)),
        dma((2, N_Y)), dma((2, N_Y)),
        dma((5, 2, 4)), dma((5, 2, 4)),
        dma((N_Y,)), dma((N_Y,)),
        dma((2,)), dma((2,)),
    ]
    outs = pl.pallas_call(
        kernel,
        out_shape=(
            shape((TOK, D), BF), shape((8, TOK), BF),
            shape((UNIT, FF), BF), shape((UNIT, FF), BF), shape((DOWN, D), BF),
        ),
        in_specs=[anywhere] * 7,
        out_specs=(anywhere,) * 5,
        scratch_shapes=scratch,
        compiler_params=pltpu.CompilerParams(
            collective_id=0, has_side_effects=True, vmem_limit_bytes=60 * 1024 * 1024
        ),
    )(tokens, out_grad, routes.T, gate_values.T, w_gate, w_up, w_down)
    return pl.pallas_call(
        hand_over,
        out_shape=(
            shape((TOK, D), BF), shape((8, TOK), BF),
            shape((1, UNIT, FF), BF), shape((1, UNIT, FF), BF), shape((1, DOWN, D), BF),
        ),
        in_specs=[vmem] * 5,
        out_specs=(vmem,) * 5,
    )(*outs)


def solution(mesh):
    rows = P(("dp", "expert"), None)
    weight = P("expert", "dp", None)

    def whole(*args):
        token_grad, gate_grad, wg, wu, wd = body(*args)
        return token_grad, gate_grad.T, wg, wu, wd

    return jax.shard_map(
        whole,
        mesh=mesh,
        in_specs=(rows,) * 4 + (weight,) * 3,
        out_specs=(rows, rows, weight, weight, weight),
        check_vma=False,
    )
```

```python
import jax
import jax.numpy as jnp
from jax import lax
from jax.experimental import pallas as pl
from jax.experimental.pallas import tpu as pltpu
from jax.sharding import PartitionSpec as P

EXP_DEV = 8
MESH = pl.DeviceIdType.MESH
BF = jnp.bfloat16
F32 = jnp.float32
ROWS = (((0,), (0,)), ((), ()))
LAST = (((1,), (1,)), ((), ()))

N_E = 16
N_Y = 8
TOK = 128
CAP = 16
SLOTS = N_E * CAP
D = 1280
FF = 512
UNIT = 40
DOWN = 16
PEERS = (8, 7, 9, 6, 10, 5, 11, 4, 12, 3, 13, 2, 14, 1, 15)
STEPS = ((4, 3), (3, 4), (4, 3))
PARTS = ((3, 3), (3, 3), (3, 4), (3, 4), (3, 4))
LAST_IN = 3


def kernel(
    tokens_hbm, grads_hbm, routes_hbm, gates_hbm, wg_hbm, wu_hbm, wd_hbm,
    tok_hbm, gate_hbm, wg_out_hbm, wu_out_hbm, wd_out_hbm,
    tok_out, gate_out, wg_out, wu_out, wd_out,
    tokens, grads, routes, gates,
    place_ref, send_x, send_g, send_s, got_x, got_g, got_s, ret, back, ret_s, back_s,
    w_all, wdn, w_mat, xt_ref, wdt_ref,
    hu_ref, g_ref, a_ref, dhu_ref, e_ref,
    d2, dd, s2, sd, snd2, sndd, rec2, recd, xq_out, xq_in, xw_out, xw_in, far_out, far_in,
    loc, ss, rs, sx, rx, sg, rg, sr, rr, sxw, rxw, sxd, rxd, sag, rag, ssw, rsw,
    ssd, rsd, srs, rrs, sxq, rxq, sxr, rxr, sfr, rfr, st, rt,
):
    dp = lax.axis_index("dp")
    ex = lax.axis_index("expert")
    core = lax.rem(dp, 2)
    xh = lax.rem(lax.div(dp, 2), 2)
    y = lax.div(dp, 4)
    other = 1 - core
    across = 1 - xh
    low = lax.rem(dp, 4)
    sibling = (dp + 1 - 2 * core, ex)
    partner = (dp + 2 - 4 * xh, ex)
    ups = (
        (lax.rem(y + 1, N_Y) * 4 + low, ex),
        (lax.rem(y + N_Y - 1, N_Y) * 4 + low, ex),
    )

    up_two = (lax.rem(y + 2, N_Y) * 4 + low, ex)
    down_two = (lax.rem(y + N_Y - 2, N_Y) * 4 + low, ex)

    def wrap(offset):
        return lax.rem(y + (offset + 2 * N_Y), N_Y)

    def peer(k):
        return lax.rem(ex + (k + N_E), N_E)

    started = []

    def go(src, dst, send, recv, to):
        copy = pltpu.make_async_remote_copy(
            src_ref=src, dst_ref=dst, send_sem=send, recv_sem=recv,
            device_id=to, device_id_type=MESH,
        )
        copy.start()
        started.append(copy)
        return copy

    leaving = []

    def leave(i, src, dst):
        leaving.append(pltpu.make_async_copy(src, dst, loc.at[7 + i]))
        leaving[-1].start()

    barrier = pltpu.get_barrier_semaphore()
    for to in (sibling, partner, down_two) + ups:
        pl.semaphore_signal(barrier, inc=1, device_id=to, device_id_type=MESH)
    for k in range(1, N_E):
        pl.semaphore_signal(barrier, inc=1, device_id=(dp, peer(k)), device_id_type=MESH)

    local = []
    for i, (src, dst) in enumerate((
        (routes_hbm, routes), (gates_hbm, gates), (tokens_hbm, tokens),
        (wg_hbm.at[0], w_all.at[y, xh, core, :, pl.ds(0, FF)]),
        (wu_hbm.at[0], w_all.at[y, xh, core, :, pl.ds(FF, FF)]),
        (wd_hbm.at[0], wdn.at[y, xh, core]), (grads_hbm, grads),
    )):
        local.append(pltpu.make_async_copy(src, dst, loc.at[i]))
        local[-1].start()

    expert_id = EXP_DEV * lax.broadcasted_iota(jnp.int32, (N_E, CAP, TOK), 0).reshape(SLOTS, TOK)
    slot_id = lax.broadcasted_iota(jnp.int32, (N_E, CAP, TOK), 1).reshape(SLOTS, TOK)
    before = (
        lax.broadcasted_iota(jnp.int32, (TOK, TOK), 0)
        < lax.broadcasted_iota(jnp.int32, (TOK, TOK), 1)
    )
    before = jnp.where(before, 1.0, 0.0).astype(BF)
    local[0].wait()
    route = routes[...]
    chosen = jnp.zeros((SLOTS, TOK), F32)
    for k in range(8):
        match = route[k : k + 1] == expert_id
        chosen = jnp.where(match, 1.0, chosen)
    rank = jnp.dot(chosen.astype(BF), before, preferred_element_type=F32)
    placing = jnp.where(rank == slot_id.astype(F32), chosen, 0.0)
    placing = placing.astype(BF)
    local[2].wait()
    send_x[...] = (
        jnp.dot(placing, tokens[...], preferred_element_type=F32)
        .astype(BF).reshape(N_E, CAP, D)
    )

    pl.semaphore_wait(barrier, 5 + N_E - 1)

    row_x = [
        go(send_x.at[peer(k)], got_x.at[ex], sx.at[k], rx.at[k], (dp, peer(k)))
        for k in PEERS
    ]
    for i in range(3, 6):
        local[i].wait()

    def block(piece, at):
        if piece < 2:
            return w_all.at[at, xh if piece == 0 else across, core]
        return wdn.at[at, xh if piece == 2 else across, core]

    def ring_send(piece, way, step):
        at = block(piece, wrap(-step if way == 0 else step))
        return go(at, at, sag.at[piece, way, step], rag.at[piece, way, step], ups[way])

    shared = []

    def to_sibling(piece, offset, index):
        at = block(piece, wrap(offset))
        shared.append(go(at, at, ssw.at[piece, index], rsw.at[piece, index], sibling))

    def to_partner(offset, index):
        at = block(2, wrap(offset))
        return go(at, at, sxd.at[index], rxd.at[index], partner)

    ring = {}
    crossed = {}
    for way in range(2):
        ring[0, way] = ring_send(0, way, 0)
    mine = block(0, y)
    part = go(mine, mine, sxw, rxw, partner)
    for way in range(2):
        ring[2, way] = ring_send(2, way, 0)
    crossed[0] = to_partner(0, 0)
    to_sibling(0, 0, 0)
    to_sibling(2, 0, 0)
    got_x[ex] = send_x[ex]
    place_ref[...] = placing
    local[1].wait()
    gate_wide = gates[...].astype(F32)
    gate_tok = jnp.zeros((SLOTS, TOK), F32)
    for k in range(8):
        gate_tok = jnp.where(route[k : k + 1] == expert_id, gate_wide[k : k + 1], gate_tok)
    gate_column = jnp.sum(placing.astype(F32) * gate_tok, axis=1, keepdims=True)
    gate_rows = jnp.broadcast_to(gate_column, (SLOTS, 128)).reshape(N_E, CAP, 128)
    diagonal = (
        lax.broadcasted_iota(jnp.int32, (CAP, 128), 0)
        == lax.broadcasted_iota(jnp.int32, (CAP, 128), 1)
    )
    send_s[...] = jnp.sum(jnp.where(diagonal[None], gate_rows, 0.0), axis=1, keepdims=True)
    row_s = [
        go(send_s.at[peer(k)], got_s.at[ex], ss.at[k], rs.at[k], (dp, peer(k)))
        for k in PEERS
    ]
    got_s[ex] = send_s[ex]

    local[6].wait()
    send_g[...] = (
        jnp.dot(placing, grads[...], preferred_element_type=F32)
        .astype(BF).reshape(N_E, CAP, D)
    )
    got_g[ex] = send_g[ex]

    part.wait_recv()
    for way in range(2):
        ring[1, way] = ring_send(1, way, 0)
    row_g = [
        go(send_g.at[peer(k)], got_g.at[ex], sg.at[k], rg.at[k], (dp, peer(k)))
        for k in PEERS
    ]
    to_sibling(1, 0, 0)

    late = [(0, 0)]
    for turn_at in range(5):
        fresh = []
        for piece in (0, 2, 1):
            step = turn_at - 1 if piece == 1 else turn_at
            for way in range(2):
                if 0 <= step < STEPS[piece][way]:
                    ring[piece, way].wait_recv()
                    if step + 1 < STEPS[piece][way]:
                        ring[piece, way] = ring_send(piece, way, step + 1)
                    offset = -1 - step if way == 0 else 1 + step
                    index = 1 + step if way == 0 else 1 + STEPS[piece][0] + step
                    if piece == 2:
                        crossed[index] = to_partner(offset, index)
                        fresh.append((offset, index))
                    to_sibling(piece, offset, index)
        for offset, index in late:
            crossed[index].wait_recv()
            to_sibling(3, offset, index)
        late = fresh
    for offset, index in late:
        crossed[index].wait_recv()
        to_sibling(3, offset, index)
    for copy in shared:
        copy.wait_recv()

    def flatten(i, carry):
        at = pl.ds(pl.multiple_of(i * 4 * UNIT, 4 * UNIT), 4 * UNIT)
        w_mat[at] = w_all[i].astype(F32).reshape(4 * UNIT, 2 * FF).astype(BF)
        return carry

    lax.fori_loop(0, N_Y, flatten, 0)
    for copy in row_x:
        copy.wait_recv()
    rows = got_x[...].reshape(SLOTS, D)
    hu_ref[...] = jnp.dot(rows, w_mat[...], preferred_element_type=F32)
    xt_ref[...] = rows.T
    wdt_ref[...] = wdn[...].reshape(FF, D).T
    for copy in row_s:
        copy.wait_recv()

    def act_grad(sources):
        got = jnp.concatenate([got_g[i] for i in sources], axis=0)
        g = jnp.dot(got, wdt_ref[...], preferred_element_type=F32)
        for n, i in enumerate(sources):
            g_ref[pl.ds(pl.multiple_of(i * CAP, CAP), CAP)] = g[n * CAP : (n + 1) * CAP]

    def elementwise(i):
        at = pl.ds(pl.multiple_of(i * CAP, CAP), CAP)
        h, u, g = hu_ref[at, :FF], hu_ref[at, FF:], g_ref[at]
        gate = jnp.sum(
            jnp.where(diagonal, jnp.broadcast_to(got_s[i], (CAP, 128)), 0.0),
            axis=1, keepdims=True,
        )
        s = jax.nn.sigmoid(h)
        a = (h * s * u).astype(BF)
        a_ref[at] = a
        term = jnp.sum(a.astype(F32) * g, axis=1, keepdims=True)
        ret_s[i] = jnp.sum(
            jnp.where(diagonal, jnp.broadcast_to(term, (CAP, 128)), 0.0), axis=0, keepdims=True
        )
        g = gate * g
        dhu_ref[at, :FF] = (g * u * s * (1.0 + h * (1.0 - s))).astype(BF)
        dhu_ref[at, FF:] = (g * h * s).astype(BF)
        e_ref[at] = (gate * got_g[i].astype(F32)).astype(BF)

    def turn(n, carry):
        k = 8 + lax.div(n + 1, 2) * (1 - 2 * lax.rem(n, 2))
        elementwise(lax.rem(ex + N_E - k, N_E))
        return carry

    early = N_E - 1 - LAST_IN
    for copy in row_g[:early]:
        copy.wait_recv()
    act_grad([ex] + [peer(-k) for k in PEERS[:early]])
    elementwise(ex)
    lax.fori_loop(0, early, turn, 0)
    for copy in row_g[early:]:
        copy.wait_recv()
    act_grad([peer(-k) for k in PEERS[early:]])
    lax.fori_loop(early, N_E - 1, turn, 0)

    given = {}
    partial, paired = (d2, dd), (s2, sd)

    def give(kind, offset):
        at = wrap(offset)
        index = offset % N_Y
        given[kind, index] = go(
            partial[kind].at[at, :, other], paired[kind].at[at],
            ssd.at[kind, index], rsd.at[kind, index], sibling,
        )

    order = (4, 3, -3, 2, -2, 1, -1, 0)
    dd[...] = (
        lax.dot_general(a_ref[...], e_ref[...], ROWS, preferred_element_type=F32)
        .astype(BF).reshape(N_Y, 2, 2, DOWN, D)
    )
    for offset in order:
        give(1, offset)
    for offset in order:
        at = wrap(offset)
        d2[at] = (
            jnp.dot(
                xt_ref[pl.ds(pl.multiple_of(at * 4 * UNIT, 4 * UNIT), 4 * UNIT)], dhu_ref[...],
                preferred_element_type=F32,
            ).reshape(2, 2, UNIT, 2 * FF).astype(BF)
        )
        give(0, offset)

    arrived = set()

    def chip_sum(kind, offset, half, lanes=slice(None)):
        index = offset % N_Y
        if (kind, index) not in arrived:
            arrived.add((kind, index))
            given[kind, index].wait_recv()
        at = wrap(offset)
        own, came = partial[kind], paired[kind]
        return own[at, half, core, :, lanes].astype(F32) + came[at, half, :, lanes].astype(F32)

    def send_buf(piece, way, step):
        return snd2.at[piece, way, step] if piece < 4 else sndd.at[way, step]

    def recv_buf(piece, way, step):
        return rec2.at[piece, way, step] if piece < 4 else recd.at[way, step]

    going = {}
    swapped = {}

    def own_term(piece, offset):
        if piece < 4:
            lanes = slice(0, FF) if piece % 2 == 0 else slice(FF, 2 * FF)
            return chip_sum(0, offset, across if piece < 2 else xh, lanes)
        swapped[offset % N_Y].wait_recv()
        return chip_sum(1, offset, xh) + xq_in[offset % N_Y].astype(F32)

    def reduce_step(piece, way, step):
        left = PARTS[piece][way] - step
        total = own_term(piece, left if way == 0 else -left)
        if step > 0:
            going[piece, way].wait_recv()
            total = total + recv_buf(piece, way, step - 1)[...].astype(F32)
        if piece < 2 and way == 0 and step == 1:
            far[piece].wait_recv()
            total = total + far_in[piece].astype(F32)
        src = send_buf(piece, way, step)
        src[...] = total.astype(BF)
        going[piece, way] = go(
            src, recv_buf(piece, way, step),
            srs.at[piece, way, step], rrs.at[piece, way, step], ups[way],
        )

    far = []
    for piece in range(2):
        lanes = slice(piece * FF, piece * FF + FF)
        far_out[piece] = chip_sum(0, 4, across, lanes).astype(BF)
        far.append(go(far_out.at[piece], far_in.at[piece], sfr.at[piece], rfr.at[piece], up_two))
        for way in range(2):
            reduce_step(piece, way, 0)
    for offset in (3, -4, 2, -3, 1, -2, -1, 0):
        index = offset % N_Y
        xq_out[index] = chip_sum(1, offset, across).astype(BF)
        swapped[index] = go(
            xq_out.at[index], xq_in.at[index], sxq.at[index], rxq.at[index], partner
        )
    for piece in range(2, 4):
        for way in range(2):
            reduce_step(piece, way, 0)
    ret[...] = (
        lax.dot_general(dhu_ref[...], w_mat[...], LAST, preferred_element_type=F32)
        .astype(BF).reshape(N_E, CAP, D)
    )
    back_rows = [
        go(ret.at[peer(k)], back.at[ex], sr.at[k], rr.at[k], (dp, peer(k)))
        for k in PEERS
    ]
    back_terms = [
        go(ret_s.at[peer(k)], back_s.at[ex], st.at[k], rt.at[k], (dp, peer(k)))
        for k in PEERS
    ]
    back[ex] = ret[ex]
    back_s[ex] = ret_s[ex]
    def ring_total(piece):
        total = own_term(piece, 0)
        for way in range(2):
            going[piece, way].wait_recv()
            total = total + recv_buf(piece, way, PARTS[piece][way] - 1)[...].astype(F32)
        return total

    crossing = []
    for step in range(4):
        if step == 3:
            for piece in range(2):
                xw_out[piece] = ring_total(piece).astype(BF)
                crossing.append(
                    go(xw_out.at[piece], xw_in.at[piece], sxr.at[piece], rxr.at[piece], partner)
                )
        for piece in range(4):
            for way in range(2):
                if 0 < step < PARTS[piece][way]:
                    reduce_step(piece, way, step)
        for way in range(2):
            if step < PARTS[4][way]:
                reduce_step(4, way, step)

    kept = [ring_total(2), ring_total(3)]
    wd_out[...] = ring_total(4).astype(BF)
    leave(4, wd_out, wd_out_hbm)

    for copy in back_rows + back_terms:
        copy.wait_recv()
    place = place_ref[...]
    tok_out[...] = lax.dot_general(
        place, back[...].reshape(SLOTS, D), ROWS, preferred_element_type=F32
    ).astype(BF)
    leave(0, tok_out, tok_hbm)
    terms = jnp.sum(
        jnp.where(diagonal[None], jnp.broadcast_to(back_s[...], (N_E, CAP, 128)), 0.0),
        axis=2, keepdims=True,
    )
    pick = (
        lax.broadcasted_iota(jnp.int32, (N_E, CAP, 128), 0)
        == lax.broadcasted_iota(jnp.int32, (N_E, CAP, 128), 2)
    )
    terms = jnp.where(pick, jnp.broadcast_to(terms, (N_E, CAP, 128)), 0.0)
    terms = terms.reshape(SLOTS, 128).astype(BF)
    by_expert = lax.dot_general(terms, place, ROWS, preferred_element_type=F32)[:N_E]
    ids = lax.broadcasted_iota(jnp.int32, (N_E, TOK), 0) * EXP_DEV
    line = lax.broadcasted_iota(jnp.int32, (8, TOK), 0)
    result = jnp.zeros((8, TOK), F32)
    route = routes[...]
    for k in range(8):
        value = jnp.sum(
            jnp.where(route[k : k + 1] == ids, by_expert, 0.0), axis=0, keepdims=True
        )
        result = jnp.where(line == k, value, result)
    gate_out[...] = result.astype(BF)
    leave(1, gate_out, gate_hbm)

    for piece, out in enumerate((wg_out, wu_out)):
        crossing[piece].wait_recv()
        out[...] = (kept[piece] + xw_in[piece].astype(F32)).astype(BF)
    leave(2, wg_out, wg_out_hbm)
    leave(3, wu_out, wu_out_hbm)
    for copy in leaving:
        copy.wait()
    for copy in started:
        copy.wait_send()


def hand_over(*refs):
    for i in range(5):
        refs[5 + i][...] = refs[i][...].reshape(refs[5 + i].shape)


def body(tokens, out_grad, routes, gate_values, w_gate, w_up, w_down):
    anywhere = pl.BlockSpec(memory_space=pl.ANY)
    vmem = pl.BlockSpec(memory_space=pltpu.VMEM)
    dma = pltpu.SemaphoreType.DMA
    shape = jax.ShapeDtypeStruct
    scratch = [
        pltpu.VMEM((TOK, D), BF),
        pltpu.VMEM((8, TOK), BF),
        pltpu.VMEM((UNIT, FF), BF),
        pltpu.VMEM((UNIT, FF), BF),
        pltpu.VMEM((DOWN, D), BF),
        pltpu.VMEM((TOK, D), BF),
        pltpu.VMEM((TOK, D), BF),
        pltpu.VMEM((8, TOK), jnp.int32),
        pltpu.VMEM((8, TOK), BF),
        pltpu.VMEM((SLOTS, TOK), BF),
        pltpu.VMEM((N_E, CAP, D), BF),
        pltpu.VMEM((N_E, CAP, D), BF),
        pltpu.VMEM((N_E, 1, 128), F32),
        pltpu.VMEM((N_E, CAP, D), BF),
        pltpu.VMEM((N_E, CAP, D), BF),
        pltpu.VMEM((N_E, 1, 128), F32),
        pltpu.VMEM((N_E, CAP, D), BF),
        pltpu.VMEM((N_E, CAP, D), BF),
        pltpu.VMEM((N_E, 1, 128), F32),
        pltpu.VMEM((N_E, 1, 128), F32),
        pltpu.VMEM((N_Y, 2, 2, UNIT, 2 * FF), BF),
        pltpu.VMEM((N_Y, 2, 2, DOWN, D), BF),
        pltpu.VMEM((D, 2 * FF), BF),
        pltpu.VMEM((D, SLOTS), BF),
        pltpu.VMEM((D, FF), BF),
        pltpu.VMEM((SLOTS, 2 * FF), F32),
        pltpu.VMEM((SLOTS, FF), F32),
        pltpu.VMEM((SLOTS, FF), BF),
        pltpu.VMEM((SLOTS, 2 * FF), BF),
        pltpu.VMEM((SLOTS, D), BF),
        pltpu.VMEM((N_Y, 2, 2, UNIT, 2 * FF), BF),
        pltpu.VMEM((N_Y, 2, 2, DOWN, D), BF),
        pltpu.VMEM((N_Y, 2, UNIT, 2 * FF), BF),
        pltpu.VMEM((N_Y, 2, DOWN, D), BF),
        pltpu.VMEM((4, 2, 4, UNIT, FF), BF),
        pltpu.VMEM((2, 4, DOWN, D), BF),
        pltpu.VMEM((4, 2, 4, UNIT, FF), BF),
        pltpu.VMEM((2, 4, DOWN, D), BF),
        pltpu.VMEM((N_Y, DOWN, D), BF),
        pltpu.VMEM((N_Y, DOWN, D), BF),
        pltpu.VMEM((2, UNIT, FF), BF),
        pltpu.VMEM((2, UNIT, FF), BF),
        pltpu.VMEM((2, UNIT, FF), BF),
        pltpu.VMEM((2, UNIT, FF), BF),
        dma((12,)),
        dma((N_E,)), dma((N_E,)), dma((N_E,)), dma((N_E,)),
        dma((N_E,)), dma((N_E,)), dma((N_E,)), dma((N_E,)),
        dma, dma,
        dma((N_Y,)), dma((N_Y,)),
        dma((3, 2, 4)), dma((3, 2, 4)),
        dma((4, N_Y)), dma((4, N_Y)),
        dma((2, N_Y)), dma((2, N_Y)),
        dma((5, 2, 4)), dma((5, 2, 4)),
        dma((N_Y,)), dma((N_Y,)),
        dma((2,)), dma((2,)),
        dma((2,)), dma((2,)),
        dma((N_E,)), dma((N_E,)),
    ]
    outs = pl.pallas_call(
        kernel,
        out_shape=(
            shape((TOK, D), BF), shape((8, TOK), BF),
            shape((UNIT, FF), BF), shape((UNIT, FF), BF), shape((DOWN, D), BF),
        ),
        in_specs=[anywhere] * 7,
        out_specs=(anywhere,) * 5,
        scratch_shapes=scratch,
        compiler_params=pltpu.CompilerParams(
            collective_id=0, has_side_effects=True, vmem_limit_bytes=60 * 1024 * 1024
        ),
    )(tokens, out_grad, routes.T, gate_values.T, w_gate, w_up, w_down)
    return pl.pallas_call(
        hand_over,
        out_shape=(
            shape((TOK, D), BF), shape((8, TOK), BF),
            shape((1, UNIT, FF), BF), shape((1, UNIT, FF), BF), shape((1, DOWN, D), BF),
        ),
        in_specs=[vmem] * 5,
        out_specs=(vmem,) * 5,
    )(*outs)


def solution(mesh):
    rows = P(("dp", "expert"), None)
    weight = P("expert", "dp", None)

    def whole(*args):
        token_grad, gate_grad, wg, wu, wd = body(*args)
        return token_grad, gate_grad.T, wg, wu, wd

    return jax.shard_map(
        whole,
        mesh=mesh,
        in_specs=(rows,) * 4 + (weight,) * 3,
        out_specs=(rows, rows, weight, weight, weight),
        check_vma=False,
    )
```

```python
import jax
import jax.numpy as jnp
from jax import lax
from jax.experimental import pallas as pl
from jax.experimental.pallas import tpu as pltpu
from jax.sharding import PartitionSpec as P

EXP_DEV = 8
MESH = pl.DeviceIdType.MESH
BF = jnp.bfloat16
F32 = jnp.float32
ROWS = (((0,), (0,)), ((), ()))
LAST = (((1,), (1,)), ((), ()))

N_E = 16
N_Y = 8
TOK = 128
CAP = 16
SLOTS = N_E * CAP
D = 1280
FF = 512
UNIT = 40
DOWN = 16
PEERS = (8, 7, 9, 6, 10, 5, 11, 4, 12, 3, 13, 2, 14, 1, 15)
STEPS = ((4, 3), (3, 4), (4, 3))
PARTS = ((3, 3), (3, 3), (3, 4), (3, 4), (3, 4))
LAST_IN = 3


def kernel(
    tokens_hbm, grads_hbm, routes_hbm, gates_hbm, wg_hbm, wu_hbm, wd_hbm,
    tok_hbm, gate_hbm, wg_out_hbm, wu_out_hbm, wd_out_hbm,
    tok_out, gate_out, wg_out, wu_out, wd_out,
    tokens, grads, routes, gates,
    place_ref, send_x, send_g, send_s, got_x, got_g, got_s, ret, back, ret_s, back_s,
    w_all, wdn, w_mat, xt_ref, wdt_ref,
    hu_ref, g_ref, a_ref, dhu_ref, e_ref,
    d2, dd, s2, sd, snd2, sndd, rec2, recd, xq_out, xq_in, xw_out, xw_in, far_out, far_in,
    loc, ss, rs, sx, rx, sg, rg, sr, rr, sxw, rxw, sxd, rxd, sag, rag, ssw, rsw,
    ssd, rsd, srs, rrs, sxq, rxq, sxr, rxr, sfr, rfr, st, rt,
):
    dp = lax.axis_index("dp")
    ex = lax.axis_index("expert")
    core = lax.rem(dp, 2)
    xh = lax.rem(lax.div(dp, 2), 2)
    y = lax.div(dp, 4)
    other = 1 - core
    across = 1 - xh
    low = lax.rem(dp, 4)
    sibling = (dp + 1 - 2 * core, ex)
    partner = (dp + 2 - 4 * xh, ex)
    ups = (
        (lax.rem(y + 1, N_Y) * 4 + low, ex),
        (lax.rem(y + N_Y - 1, N_Y) * 4 + low, ex),
    )

    up_two = (lax.rem(y + 2, N_Y) * 4 + low, ex)
    down_two = (lax.rem(y + N_Y - 2, N_Y) * 4 + low, ex)

    def wrap(offset):
        return lax.rem(y + (offset + 2 * N_Y), N_Y)

    def peer(k):
        return lax.rem(ex + (k + N_E), N_E)

    started = []

    def go(src, dst, send, recv, to):
        copy = pltpu.make_async_remote_copy(
            src_ref=src, dst_ref=dst, send_sem=send, recv_sem=recv,
            device_id=to, device_id_type=MESH,
        )
        copy.start()
        started.append(copy)
        return copy

    leaving = []

    def leave(i, src, dst):
        leaving.append(pltpu.make_async_copy(src, dst, loc.at[7 + i]))
        leaving[-1].start()

    barrier = pltpu.get_barrier_semaphore()
    for to in (sibling, partner, down_two) + ups:
        pl.semaphore_signal(barrier, inc=1, device_id=to, device_id_type=MESH)
    for k in range(1, N_E):
        pl.semaphore_signal(barrier, inc=1, device_id=(dp, peer(k)), device_id_type=MESH)

    local = []
    for i, (src, dst) in enumerate((
        (routes_hbm, routes), (gates_hbm, gates), (tokens_hbm, tokens),
        (wg_hbm.at[0], w_all.at[y, xh, core, :, pl.ds(0, FF)]),
        (wu_hbm.at[0], w_all.at[y, xh, core, :, pl.ds(FF, FF)]),
        (wd_hbm.at[0], wdn.at[y, xh, core]), (grads_hbm, grads),
    )):
        local.append(pltpu.make_async_copy(src, dst, loc.at[i]))
        local[-1].start()

    expert_id = EXP_DEV * lax.broadcasted_iota(jnp.int32, (N_E, CAP, TOK), 0).reshape(SLOTS, TOK)
    slot_id = lax.broadcasted_iota(jnp.int32, (N_E, CAP, TOK), 1).reshape(SLOTS, TOK)
    before = (
        lax.broadcasted_iota(jnp.int32, (TOK, TOK), 0)
        < lax.broadcasted_iota(jnp.int32, (TOK, TOK), 1)
    )
    before = jnp.where(before, 1.0, 0.0).astype(BF)
    local[0].wait()
    route = routes[...]
    chosen = jnp.zeros((SLOTS, TOK), F32)
    for k in range(8):
        match = route[k : k + 1] == expert_id
        chosen = jnp.where(match, 1.0, chosen)
    rank = jnp.dot(chosen.astype(BF), before, preferred_element_type=F32)
    placing = jnp.where(rank == slot_id.astype(F32), chosen, 0.0)
    placing = placing.astype(BF)
    local[2].wait()
    send_x[...] = (
        jnp.dot(placing, tokens[...], preferred_element_type=F32)
        .astype(BF).reshape(N_E, CAP, D)
    )

    pl.semaphore_wait(barrier, 5 + N_E - 1)

    row_x = [
        go(send_x.at[peer(k)], got_x.at[ex], sx.at[k], rx.at[k], (dp, peer(k)))
        for k in PEERS
    ]
    for i in range(3, 6):
        local[i].wait()

    def block(piece, at):
        if piece < 2:
            return w_all.at[at, xh if piece == 0 else across, core]
        return wdn.at[at, xh if piece == 2 else across, core]

    def ring_send(piece, way, step):
        at = block(piece, wrap(-step if way == 0 else step))
        return go(at, at, sag.at[piece, way, step], rag.at[piece, way, step], ups[way])

    shared = []

    def to_sibling(piece, offset, index):
        at = block(piece, wrap(offset))
        shared.append(go(at, at, ssw.at[piece, index], rsw.at[piece, index], sibling))

    def to_partner(offset, index):
        at = block(2, wrap(offset))
        return go(at, at, sxd.at[index], rxd.at[index], partner)

    ring = {}
    crossed = {}
    for way in range(2):
        ring[0, way] = ring_send(0, way, 0)
    mine = block(0, y)
    part = go(mine, mine, sxw, rxw, partner)
    for way in range(2):
        ring[2, way] = ring_send(2, way, 0)
    crossed[0] = to_partner(0, 0)
    to_sibling(0, 0, 0)
    to_sibling(2, 0, 0)
    got_x[ex] = send_x[ex]
    place_ref[...] = placing
    local[1].wait()
    gate_wide = gates[...].astype(F32)
    gate_tok = jnp.zeros((SLOTS, TOK), F32)
    for k in range(8):
        gate_tok = jnp.where(route[k : k + 1] == expert_id, gate_wide[k : k + 1], gate_tok)
    gate_column = jnp.sum(placing.astype(F32) * gate_tok, axis=1, keepdims=True)
    gate_rows = jnp.broadcast_to(gate_column, (SLOTS, 128)).reshape(N_E, CAP, 128)
    diagonal = (
        lax.broadcasted_iota(jnp.int32, (CAP, 128), 0)
        == lax.broadcasted_iota(jnp.int32, (CAP, 128), 1)
    )
    send_s[...] = jnp.sum(jnp.where(diagonal[None], gate_rows, 0.0), axis=1, keepdims=True)
    row_s = [
        go(send_s.at[peer(k)], got_s.at[ex], ss.at[k], rs.at[k], (dp, peer(k)))
        for k in PEERS
    ]
    got_s[ex] = send_s[ex]

    local[6].wait()
    send_g[...] = (
        jnp.dot(placing, grads[...], preferred_element_type=F32)
        .astype(BF).reshape(N_E, CAP, D)
    )
    got_g[ex] = send_g[ex]

    part.wait_recv()
    for way in range(2):
        ring[1, way] = ring_send(1, way, 0)
    row_g = [
        go(send_g.at[peer(k)], got_g.at[ex], sg.at[k], rg.at[k], (dp, peer(k)))
        for k in PEERS
    ]
    to_sibling(1, 0, 0)

    late = [(0, 0)]
    for turn_at in range(5):
        fresh = []
        for piece in (0, 2, 1):
            step = turn_at - 1 if piece == 1 else turn_at
            for way in range(2):
                if 0 <= step < STEPS[piece][way]:
                    ring[piece, way].wait_recv()
                    if step + 1 < STEPS[piece][way]:
                        ring[piece, way] = ring_send(piece, way, step + 1)
                    offset = -1 - step if way == 0 else 1 + step
                    index = 1 + step if way == 0 else 1 + STEPS[piece][0] + step
                    if piece == 2:
                        crossed[index] = to_partner(offset, index)
                        fresh.append((offset, index))
                    to_sibling(piece, offset, index)
        for offset, index in late:
            crossed[index].wait_recv()
            to_sibling(3, offset, index)
        late = fresh
    for offset, index in late:
        crossed[index].wait_recv()
        to_sibling(3, offset, index)
    for copy in shared:
        copy.wait_recv()

    def flatten(i, carry):
        at = pl.ds(pl.multiple_of(i * 4 * UNIT, 4 * UNIT), 4 * UNIT)
        w_mat[at] = w_all[i].astype(F32).reshape(4 * UNIT, 2 * FF).astype(BF)
        return carry

    lax.fori_loop(0, N_Y, flatten, 0)
    for copy in row_x:
        copy.wait_recv()
    rows = got_x[...].reshape(SLOTS, D)
    hu_ref[...] = jnp.dot(rows, w_mat[...], preferred_element_type=F32)
    xt_ref[...] = rows.T
    wdt_ref[...] = wdn[...].reshape(FF, D).T
    for copy in row_s:
        copy.wait_recv()

    def act_grad(sources):
        got = jnp.concatenate([got_g[i] for i in sources], axis=0)
        g = jnp.dot(got, wdt_ref[...], preferred_element_type=F32)
        for n, i in enumerate(sources):
            g_ref[pl.ds(pl.multiple_of(i * CAP, CAP), CAP)] = g[n * CAP : (n + 1) * CAP]

    def elementwise(i):
        at = pl.ds(pl.multiple_of(i * CAP, CAP), CAP)
        h, u, g = hu_ref[at, :FF], hu_ref[at, FF:], g_ref[at]
        gate = jnp.sum(
            jnp.where(diagonal, jnp.broadcast_to(got_s[i], (CAP, 128)), 0.0),
            axis=1, keepdims=True,
        )
        s = jax.nn.sigmoid(h)
        a = (h * s * u).astype(BF)
        a_ref[at] = a
        term = jnp.sum(a.astype(F32) * g, axis=1, keepdims=True)
        ret_s[i] = jnp.sum(
            jnp.where(diagonal, jnp.broadcast_to(term, (CAP, 128)), 0.0), axis=0, keepdims=True
        )
        g = gate * g
        dhu_ref[at, :FF] = (g * u * s * (1.0 + h * (1.0 - s))).astype(BF)
        dhu_ref[at, FF:] = (g * h * s).astype(BF)
        e_ref[at] = (gate * got_g[i].astype(F32)).astype(BF)

    def turn(n, carry):
        k = 8 + lax.div(n + 1, 2) * (1 - 2 * lax.rem(n, 2))
        elementwise(lax.rem(ex + N_E - k, N_E))
        return carry

    early = N_E - 1 - LAST_IN
    for copy in row_g[:early]:
        copy.wait_recv()
    act_grad([ex] + [peer(-k) for k in PEERS[:early]])
    elementwise(ex)
    lax.fori_loop(0, early, turn, 0)
    for copy in row_g[early:]:
        copy.wait_recv()
    act_grad([peer(-k) for k in PEERS[early:]])
    lax.fori_loop(early, N_E - 1, turn, 0)

    given = {}
    partial, paired = (d2, dd), (s2, sd)

    def give(kind, offset):
        at = wrap(offset)
        index = offset % N_Y
        given[kind, index] = go(
            partial[kind].at[at, :, other], paired[kind].at[at],
            ssd.at[kind, index], rsd.at[kind, index], sibling,
        )

    order = (4, 3, -3, 2, -2, 1, -1, 0)
    dd[...] = (
        lax.dot_general(a_ref[...], e_ref[...], ROWS, preferred_element_type=F32)
        .astype(BF).reshape(N_Y, 2, 2, DOWN, D)
    )
    for offset in order:
        give(1, offset)
    for offset in order:
        at = wrap(offset)
        d2[at] = (
            jnp.dot(
                xt_ref[pl.ds(pl.multiple_of(at * 4 * UNIT, 4 * UNIT), 4 * UNIT)], dhu_ref[...],
                preferred_element_type=F32,
            ).reshape(2, 2, UNIT, 2 * FF).astype(BF)
        )
        give(0, offset)

    arrived = set()

    def chip_sum(kind, offset, half, lanes=slice(None)):
        index = offset % N_Y
        if (kind, index) not in arrived:
            arrived.add((kind, index))
            given[kind, index].wait_recv()
        at = wrap(offset)
        own, came = partial[kind], paired[kind]
        return own[at, half, core, :, lanes].astype(F32) + came[at, half, :, lanes].astype(F32)

    def send_buf(piece, way, step):
        return snd2.at[piece, way, step] if piece < 4 else sndd.at[way, step]

    def recv_buf(piece, way, step):
        return rec2.at[piece, way, step] if piece < 4 else recd.at[way, step]

    going = {}
    swapped = {}

    def own_term(piece, offset):
        if piece < 4:
            lanes = slice(0, FF) if piece % 2 == 0 else slice(FF, 2 * FF)
            return chip_sum(0, offset, across if piece < 2 else xh, lanes)
        swapped[offset % N_Y].wait_recv()
        return chip_sum(1, offset, xh) + xq_in[offset % N_Y].astype(F32)

    def reduce_step(piece, way, step):
        left = PARTS[piece][way] - step
        total = own_term(piece, left if way == 0 else -left)
        if step > 0:
            going[piece, way].wait_recv()
            total = total + recv_buf(piece, way, step - 1)[...].astype(F32)
        if piece < 2 and way == 0 and step == 1:
            far[piece].wait_recv()
            total = total + far_in[piece].astype(F32)
        src = send_buf(piece, way, step)
        src[...] = total.astype(BF)
        going[piece, way] = go(
            src, recv_buf(piece, way, step),
            srs.at[piece, way, step], rrs.at[piece, way, step], ups[way],
        )

    for offset in (3, -4, 2, -3, 1, -2, -1, 0):
        index = offset % N_Y
        xq_out[index] = chip_sum(1, offset, across).astype(BF)
        swapped[index] = go(
            xq_out.at[index], xq_in.at[index], sxq.at[index], rxq.at[index], partner
        )
    far = []
    for piece in range(2):
        lanes = slice(piece * FF, piece * FF + FF)
        far_out[piece] = chip_sum(0, 4, across, lanes).astype(BF)
        far.append(go(far_out.at[piece], far_in.at[piece], sfr.at[piece], rfr.at[piece], up_two))
        for way in range(2):
            reduce_step(piece, way, 0)
    for piece in range(2, 4):
        for way in range(2):
            reduce_step(piece, way, 0)
    ret[...] = (
        lax.dot_general(dhu_ref[...], w_mat[...], LAST, preferred_element_type=F32)
        .astype(BF).reshape(N_E, CAP, D)
    )
    back_rows = [
        go(ret.at[peer(k)], back.at[ex], sr.at[k], rr.at[k], (dp, peer(k)))
        for k in PEERS
    ]
    back_terms = [
        go(ret_s.at[peer(k)], back_s.at[ex], st.at[k], rt.at[k], (dp, peer(k)))
        for k in PEERS
    ]
    back[ex] = ret[ex]
    back_s[ex] = ret_s[ex]
    def ring_total(piece):
        total = own_term(piece, 0)
        for way in range(2):
            going[piece, way].wait_recv()
            total = total + recv_buf(piece, way, PARTS[piece][way] - 1)[...].astype(F32)
        return total

    crossing = []
    for step in range(4):
        if step == 3:
            for piece in range(2):
                xw_out[piece] = ring_total(piece).astype(BF)
                crossing.append(
                    go(xw_out.at[piece], xw_in.at[piece], sxr.at[piece], rxr.at[piece], partner)
                )
        for piece in range(4):
            for way in range(2):
                if 0 < step < PARTS[piece][way]:
                    reduce_step(piece, way, step)
        for way in range(2):
            if step < PARTS[4][way]:
                reduce_step(4, way, step)

    kept = [ring_total(2), ring_total(3)]
    wd_out[...] = ring_total(4).astype(BF)
    leave(4, wd_out, wd_out_hbm)

    for copy in back_rows + back_terms:
        copy.wait_recv()
    place = place_ref[...]
    tok_out[...] = lax.dot_general(
        place, back[...].reshape(SLOTS, D), ROWS, preferred_element_type=F32
    ).astype(BF)
    leave(0, tok_out, tok_hbm)
    terms = jnp.sum(
        jnp.where(diagonal[None], jnp.broadcast_to(back_s[...], (N_E, CAP, 128)), 0.0),
        axis=2, keepdims=True,
    )
    pick = (
        lax.broadcasted_iota(jnp.int32, (N_E, CAP, 128), 0)
        == lax.broadcasted_iota(jnp.int32, (N_E, CAP, 128), 2)
    )
    terms = jnp.where(pick, jnp.broadcast_to(terms, (N_E, CAP, 128)), 0.0)
    terms = terms.reshape(SLOTS, 128).astype(BF)
    by_expert = lax.dot_general(terms, place, ROWS, preferred_element_type=F32)[:N_E]
    ids = lax.broadcasted_iota(jnp.int32, (N_E, TOK), 0) * EXP_DEV
    line = lax.broadcasted_iota(jnp.int32, (8, TOK), 0)
    result = jnp.zeros((8, TOK), F32)
    route = routes[...]
    for k in range(8):
        value = jnp.sum(
            jnp.where(route[k : k + 1] == ids, by_expert, 0.0), axis=0, keepdims=True
        )
        result = jnp.where(line == k, value, result)
    gate_out[...] = result.astype(BF)
    leave(1, gate_out, gate_hbm)

    for piece, out in enumerate((wg_out, wu_out)):
        crossing[piece].wait_recv()
        out[...] = (kept[piece] + xw_in[piece].astype(F32)).astype(BF)
    leave(2, wg_out, wg_out_hbm)
    leave(3, wu_out, wu_out_hbm)
    for copy in leaving:
        copy.wait()
    for copy in started:
        copy.wait_send()


def hand_over(*refs):
    for i in range(5):
        refs[5 + i][...] = refs[i][...].reshape(refs[5 + i].shape)


def body(tokens, out_grad, routes, gate_values, w_gate, w_up, w_down):
    anywhere = pl.BlockSpec(memory_space=pl.ANY)
    vmem = pl.BlockSpec(memory_space=pltpu.VMEM)
    dma = pltpu.SemaphoreType.DMA
    shape = jax.ShapeDtypeStruct
    scratch = [
        pltpu.VMEM((TOK, D), BF),
        pltpu.VMEM((8, TOK), BF),
        pltpu.VMEM((UNIT, FF), BF),
        pltpu.VMEM((UNIT, FF), BF),
        pltpu.VMEM((DOWN, D), BF),
        pltpu.VMEM((TOK, D), BF),
        pltpu.VMEM((TOK, D), BF),
        pltpu.VMEM((8, TOK), jnp.int32),
        pltpu.VMEM((8, TOK), BF),
        pltpu.VMEM((SLOTS, TOK), BF),
        pltpu.VMEM((N_E, CAP, D), BF),
        pltpu.VMEM((N_E, CAP, D), BF),
        pltpu.VMEM((N_E, 1, 128), F32),
        pltpu.VMEM((N_E, CAP, D), BF),
        pltpu.VMEM((N_E, CAP, D), BF),
        pltpu.VMEM((N_E, 1, 128), F32),
        pltpu.VMEM((N_E, CAP, D), BF),
        pltpu.VMEM((N_E, CAP, D), BF),
        pltpu.VMEM((N_E, 1, 128), F32),
        pltpu.VMEM((N_E, 1, 128), F32),
        pltpu.VMEM((N_Y, 2, 2, UNIT, 2 * FF), BF),
        pltpu.VMEM((N_Y, 2, 2, DOWN, D), BF),
        pltpu.VMEM((D, 2 * FF), BF),
        pltpu.VMEM((D, SLOTS), BF),
        pltpu.VMEM((D, FF), BF),
        pltpu.VMEM((SLOTS, 2 * FF), F32),
        pltpu.VMEM((SLOTS, FF), F32),
        pltpu.VMEM((SLOTS, FF), BF),
        pltpu.VMEM((SLOTS, 2 * FF), BF),
        pltpu.VMEM((SLOTS, D), BF),
        pltpu.VMEM((N_Y, 2, 2, UNIT, 2 * FF), BF),
        pltpu.VMEM((N_Y, 2, 2, DOWN, D), BF),
        pltpu.VMEM((N_Y, 2, UNIT, 2 * FF), BF),
        pltpu.VMEM((N_Y, 2, DOWN, D), BF),
        pltpu.VMEM((4, 2, 4, UNIT, FF), BF),
        pltpu.VMEM((2, 4, DOWN, D), BF),
        pltpu.VMEM((4, 2, 4, UNIT, FF), BF),
        pltpu.VMEM((2, 4, DOWN, D), BF),
        pltpu.VMEM((N_Y, DOWN, D), BF),
        pltpu.VMEM((N_Y, DOWN, D), BF),
        pltpu.VMEM((2, UNIT, FF), BF),
        pltpu.VMEM((2, UNIT, FF), BF),
        pltpu.VMEM((2, UNIT, FF), BF),
        pltpu.VMEM((2, UNIT, FF), BF),
        dma((12,)),
        dma((N_E,)), dma((N_E,)), dma((N_E,)), dma((N_E,)),
        dma((N_E,)), dma((N_E,)), dma((N_E,)), dma((N_E,)),
        dma, dma,
        dma((N_Y,)), dma((N_Y,)),
        dma((3, 2, 4)), dma((3, 2, 4)),
        dma((4, N_Y)), dma((4, N_Y)),
        dma((2, N_Y)), dma((2, N_Y)),
        dma((5, 2, 4)), dma((5, 2, 4)),
        dma((N_Y,)), dma((N_Y,)),
        dma((2,)), dma((2,)),
        dma((2,)), dma((2,)),
        dma((N_E,)), dma((N_E,)),
    ]
    outs = pl.pallas_call(
        kernel,
        out_shape=(
            shape((TOK, D), BF), shape((8, TOK), BF),
            shape((UNIT, FF), BF), shape((UNIT, FF), BF), shape((DOWN, D), BF),
        ),
        in_specs=[anywhere] * 7,
        out_specs=(anywhere,) * 5,
        scratch_shapes=scratch,
        compiler_params=pltpu.CompilerParams(
            collective_id=0, has_side_effects=True, vmem_limit_bytes=60 * 1024 * 1024
        ),
    )(tokens, out_grad, routes.T, gate_values.T, w_gate, w_up, w_down)
    return pl.pallas_call(
        hand_over,
        out_shape=(
            shape((TOK, D), BF), shape((8, TOK), BF),
            shape((1, UNIT, FF), BF), shape((1, UNIT, FF), BF), shape((1, DOWN, D), BF),
        ),
        in_specs=[vmem] * 5,
        out_specs=(vmem,) * 5,
    )(*outs)


def solution(mesh):
    rows = P(("dp", "expert"), None)
    weight = P("expert", "dp", None)

    def whole(*args):
        token_grad, gate_grad, wg, wu, wd = body(*args)
        return token_grad, gate_grad.T, wg, wu, wd

    return jax.shard_map(
        whole,
        mesh=mesh,
        in_specs=(rows,) * 4 + (weight,) * 3,
        out_specs=(rows, rows, weight, weight, weight),
        check_vma=False,
    )
```

```python
import jax
import jax.numpy as jnp
from jax import lax
from jax.experimental import pallas as pl
from jax.experimental.pallas import tpu as pltpu
from jax.sharding import PartitionSpec as P

EXP_DEV = 8
MESH = pl.DeviceIdType.MESH
BF = jnp.bfloat16
F32 = jnp.float32
ROWS = (((0,), (0,)), ((), ()))
LAST = (((1,), (1,)), ((), ()))

N_E = 16
N_Y = 8
TOK = 128
CAP = 16
SLOTS = N_E * CAP
D = 1280
FF = 512
UNIT = 40
DOWN = 16
PEERS = (8, 7, 9, 6, 10, 5, 11, 4, 12, 3, 13, 2, 14, 1, 15)
STEPS = ((4, 3), (3, 4), (4, 3))
PARTS = ((3, 3), (3, 3), (3, 4), (3, 4), (3, 4))
LAST_IN = 6


def kernel(
    tokens_hbm, grads_hbm, routes_hbm, gates_hbm, wg_hbm, wu_hbm, wd_hbm,
    tok_hbm, gate_hbm, wg_out_hbm, wu_out_hbm, wd_out_hbm,
    tok_out, gate_out, wg_out, wu_out, wd_out,
    tokens, grads, routes, gates,
    place_ref, send_x, send_g, send_s, got_x, got_g, got_s, ret, back, ret_s, back_s,
    w_all, wdn, w_mat, xt_ref, wdt_ref,
    hu_ref, g_ref, a_ref, dhu_ref, e_ref,
    d2, dd, s2, sd, snd2, sndd, rec2, recd, xq_out, xq_in, xw_out, xw_in, far_out, far_in,
    loc, ss, rs, sx, rx, sg, rg, sr, rr, sxw, rxw, sxd, rxd, sag, rag, ssw, rsw,
    ssd, rsd, srs, rrs, sxq, rxq, sxr, rxr, sfr, rfr, st, rt,
):
    dp = lax.axis_index("dp")
    ex = lax.axis_index("expert")
    core = lax.rem(dp, 2)
    xh = lax.rem(lax.div(dp, 2), 2)
    y = lax.div(dp, 4)
    other = 1 - core
    across = 1 - xh
    low = lax.rem(dp, 4)
    sibling = (dp + 1 - 2 * core, ex)
    partner = (dp + 2 - 4 * xh, ex)
    ups = (
        (lax.rem(y + 1, N_Y) * 4 + low, ex),
        (lax.rem(y + N_Y - 1, N_Y) * 4 + low, ex),
    )

    up_two = (lax.rem(y + 2, N_Y) * 4 + low, ex)
    down_two = (lax.rem(y + N_Y - 2, N_Y) * 4 + low, ex)

    def wrap(offset):
        return lax.rem(y + (offset + 2 * N_Y), N_Y)

    def peer(k):
        return lax.rem(ex + (k + N_E), N_E)

    started = []

    def go(src, dst, send, recv, to):
        copy = pltpu.make_async_remote_copy(
            src_ref=src, dst_ref=dst, send_sem=send, recv_sem=recv,
            device_id=to, device_id_type=MESH,
        )
        copy.start()
        started.append(copy)
        return copy

    leaving = []

    def leave(i, src, dst):
        leaving.append(pltpu.make_async_copy(src, dst, loc.at[7 + i]))
        leaving[-1].start()

    barrier = pltpu.get_barrier_semaphore()
    for to in (sibling, partner, down_two) + ups:
        pl.semaphore_signal(barrier, inc=1, device_id=to, device_id_type=MESH)
    for k in range(1, N_E):
        pl.semaphore_signal(barrier, inc=1, device_id=(dp, peer(k)), device_id_type=MESH)

    local = []
    for i, (src, dst) in enumerate((
        (routes_hbm, routes), (gates_hbm, gates), (tokens_hbm, tokens),
        (wg_hbm.at[0], w_all.at[y, xh, core, :, pl.ds(0, FF)]),
        (wu_hbm.at[0], w_all.at[y, xh, core, :, pl.ds(FF, FF)]),
        (wd_hbm.at[0], wdn.at[y, xh, core]), (grads_hbm, grads),
    )):
        local.append(pltpu.make_async_copy(src, dst, loc.at[i]))
        local[-1].start()

    expert_id = EXP_DEV * lax.broadcasted_iota(jnp.int32, (N_E, CAP, TOK), 0).reshape(SLOTS, TOK)
    slot_id = lax.broadcasted_iota(jnp.int32, (N_E, CAP, TOK), 1).reshape(SLOTS, TOK)
    before = (
        lax.broadcasted_iota(jnp.int32, (TOK, TOK), 0)
        < lax.broadcasted_iota(jnp.int32, (TOK, TOK), 1)
    )
    before = jnp.where(before, 1.0, 0.0).astype(BF)
    local[0].wait()
    route = routes[...]
    chosen = jnp.zeros((SLOTS, TOK), F32)
    for k in range(8):
        match = route[k : k + 1] == expert_id
        chosen = jnp.where(match, 1.0, chosen)
    rank = jnp.dot(chosen.astype(BF), before, preferred_element_type=F32)
    placing = jnp.where(rank == slot_id.astype(F32), chosen, 0.0)
    placing = placing.astype(BF)
    local[2].wait()
    send_x[...] = (
        jnp.dot(placing, tokens[...], preferred_element_type=F32)
        .astype(BF).reshape(N_E, CAP, D)
    )

    pl.semaphore_wait(barrier, 5 + N_E - 1)

    row_x = [
        go(send_x.at[peer(k)], got_x.at[ex], sx.at[k], rx.at[k], (dp, peer(k)))
        for k in PEERS
    ]
    for i in range(3, 6):
        local[i].wait()

    def block(piece, at):
        if piece < 2:
            return w_all.at[at, xh if piece == 0 else across, core]
        return wdn.at[at, xh if piece == 2 else across, core]

    def ring_send(piece, way, step):
        at = block(piece, wrap(-step if way == 0 else step))
        return go(at, at, sag.at[piece, way, step], rag.at[piece, way, step], ups[way])

    shared = []

    def to_sibling(piece, offset, index):
        at = block(piece, wrap(offset))
        shared.append(go(at, at, ssw.at[piece, index], rsw.at[piece, index], sibling))

    def to_partner(offset, index):
        at = block(2, wrap(offset))
        return go(at, at, sxd.at[index], rxd.at[index], partner)

    ring = {}
    crossed = {}
    for way in range(2):
        ring[0, way] = ring_send(0, way, 0)
    mine = block(0, y)
    part = go(mine, mine, sxw, rxw, partner)
    for way in range(2):
        ring[2, way] = ring_send(2, way, 0)
    crossed[0] = to_partner(0, 0)
    to_sibling(0, 0, 0)
    to_sibling(2, 0, 0)
    got_x[ex] = send_x[ex]
    place_ref[...] = placing
    local[1].wait()
    gate_wide = gates[...].astype(F32)
    gate_tok = jnp.zeros((SLOTS, TOK), F32)
    for k in range(8):
        gate_tok = jnp.where(route[k : k + 1] == expert_id, gate_wide[k : k + 1], gate_tok)
    gate_column = jnp.sum(placing.astype(F32) * gate_tok, axis=1, keepdims=True)
    gate_rows = jnp.broadcast_to(gate_column, (SLOTS, 128)).reshape(N_E, CAP, 128)
    diagonal = (
        lax.broadcasted_iota(jnp.int32, (CAP, 128), 0)
        == lax.broadcasted_iota(jnp.int32, (CAP, 128), 1)
    )
    send_s[...] = jnp.sum(jnp.where(diagonal[None], gate_rows, 0.0), axis=1, keepdims=True)
    row_s = [
        go(send_s.at[peer(k)], got_s.at[ex], ss.at[k], rs.at[k], (dp, peer(k)))
        for k in PEERS
    ]
    got_s[ex] = send_s[ex]

    local[6].wait()
    send_g[...] = (
        jnp.dot(placing, grads[...], preferred_element_type=F32)
        .astype(BF).reshape(N_E, CAP, D)
    )
    got_g[ex] = send_g[ex]

    part.wait_recv()
    for way in range(2):
        ring[1, way] = ring_send(1, way, 0)
    row_g = [
        go(send_g.at[peer(k)], got_g.at[ex], sg.at[k], rg.at[k], (dp, peer(k)))
        for k in PEERS
    ]
    to_sibling(1, 0, 0)

    late = [(0, 0)]
    for turn_at in range(5):
        fresh = []
        for piece in (0, 2, 1):
            step = turn_at - 1 if piece == 1 else turn_at
            for way in range(2):
                if 0 <= step < STEPS[piece][way]:
                    ring[piece, way].wait_recv()
                    if step + 1 < STEPS[piece][way]:
                        ring[piece, way] = ring_send(piece, way, step + 1)
                    offset = -1 - step if way == 0 else 1 + step
                    index = 1 + step if way == 0 else 1 + STEPS[piece][0] + step
                    if piece == 2:
                        crossed[index] = to_partner(offset, index)
                        fresh.append((offset, index))
                    to_sibling(piece, offset, index)
        for offset, index in late:
            crossed[index].wait_recv()
            to_sibling(3, offset, index)
        late = fresh
    for offset, index in late:
        crossed[index].wait_recv()
        to_sibling(3, offset, index)
    for copy in shared:
        copy.wait_recv()

    def flatten(i, carry):
        at = pl.ds(pl.multiple_of(i * 4 * UNIT, 4 * UNIT), 4 * UNIT)
        w_mat[at] = w_all[i].astype(F32).reshape(4 * UNIT, 2 * FF).astype(BF)
        return carry

    lax.fori_loop(0, N_Y, flatten, 0)
    for copy in row_x:
        copy.wait_recv()
    rows = got_x[...].reshape(SLOTS, D)
    hu_ref[...] = jnp.dot(rows, w_mat[...], preferred_element_type=F32)
    xt_ref[...] = rows.T
    wdt_ref[...] = wdn[...].reshape(FF, D).T
    for copy in row_s:
        copy.wait_recv()

    def act_grad(sources):
        got = jnp.concatenate([got_g[i] for i in sources], axis=0)
        g = jnp.dot(got, wdt_ref[...], preferred_element_type=F32)
        for n, i in enumerate(sources):
            g_ref[pl.ds(pl.multiple_of(i * CAP, CAP), CAP)] = g[n * CAP : (n + 1) * CAP]

    def elementwise(i):
        at = pl.ds(pl.multiple_of(i * CAP, CAP), CAP)
        h, u, g = hu_ref[at, :FF], hu_ref[at, FF:], g_ref[at]
        gate = jnp.sum(
            jnp.where(diagonal, jnp.broadcast_to(got_s[i], (CAP, 128)), 0.0),
            axis=1, keepdims=True,
        )
        s = jax.nn.sigmoid(h)
        a = (h * s * u).astype(BF)
        a_ref[at] = a
        term = jnp.sum(a.astype(F32) * g, axis=1, keepdims=True)
        ret_s[i] = jnp.sum(
            jnp.where(diagonal, jnp.broadcast_to(term, (CAP, 128)), 0.0), axis=0, keepdims=True
        )
        g = gate * g
        dhu_ref[at, :FF] = (g * u * s * (1.0 + h * (1.0 - s))).astype(BF)
        dhu_ref[at, FF:] = (g * h * s).astype(BF)
        e_ref[at] = (gate * got_g[i].astype(F32)).astype(BF)

    def turn(n, carry):
        k = 8 + lax.div(n + 1, 2) * (1 - 2 * lax.rem(n, 2))
        elementwise(lax.rem(ex + N_E - k, N_E))
        return carry

    early = N_E - 1 - LAST_IN
    for copy in row_g[:early]:
        copy.wait_recv()
    act_grad([ex] + [peer(-k) for k in PEERS[:early]])
    elementwise(ex)
    lax.fori_loop(0, early, turn, 0)
    for copy in row_g[early:]:
        copy.wait_recv()
    act_grad([peer(-k) for k in PEERS[early:]])
    lax.fori_loop(early, N_E - 1, turn, 0)

    given = {}
    partial, paired = (d2, dd), (s2, sd)

    def give(kind, offset):
        at = wrap(offset)
        index = offset % N_Y
        given[kind, index] = go(
            partial[kind].at[at, :, other], paired[kind].at[at],
            ssd.at[kind, index], rsd.at[kind, index], sibling,
        )

    order = (4, 3, -3, 2, -2, 1, -1, 0)
    dd[...] = (
        lax.dot_general(a_ref[...], e_ref[...], ROWS, preferred_element_type=F32)
        .astype(BF).reshape(N_Y, 2, 2, DOWN, D)
    )
    for offset in order:
        give(1, offset)
    for offset in order:
        at = wrap(offset)
        d2[at] = (
            jnp.dot(
                xt_ref[pl.ds(pl.multiple_of(at * 4 * UNIT, 4 * UNIT), 4 * UNIT)], dhu_ref[...],
                preferred_element_type=F32,
            ).reshape(2, 2, UNIT, 2 * FF).astype(BF)
        )
        give(0, offset)

    arrived = set()

    def chip_sum(kind, offset, half, lanes=slice(None)):
        index = offset % N_Y
        if (kind, index) not in arrived:
            arrived.add((kind, index))
            given[kind, index].wait_recv()
        at = wrap(offset)
        own, came = partial[kind], paired[kind]
        return own[at, half, core, :, lanes].astype(F32) + came[at, half, :, lanes].astype(F32)

    def send_buf(piece, way, step):
        return snd2.at[piece, way, step] if piece < 4 else sndd.at[way, step]

    def recv_buf(piece, way, step):
        return rec2.at[piece, way, step] if piece < 4 else recd.at[way, step]

    going = {}
    swapped = {}

    def own_term(piece, offset):
        if piece < 4:
            lanes = slice(0, FF) if piece % 2 == 0 else slice(FF, 2 * FF)
            return chip_sum(0, offset, across if piece < 2 else xh, lanes)
        swapped[offset % N_Y].wait_recv()
        return chip_sum(1, offset, xh) + xq_in[offset % N_Y].astype(F32)

    def reduce_step(piece, way, step):
        left = PARTS[piece][way] - step
        total = own_term(piece, left if way == 0 else -left)
        if step > 0:
            going[piece, way].wait_recv()
            total = total + recv_buf(piece, way, step - 1)[...].astype(F32)
        if piece < 2 and way == 0 and step == 1:
            far[piece].wait_recv()
            total = total + far_in[piece].astype(F32)
        src = send_buf(piece, way, step)
        src[...] = total.astype(BF)
        going[piece, way] = go(
            src, recv_buf(piece, way, step),
            srs.at[piece, way, step], rrs.at[piece, way, step], ups[way],
        )

    for offset in (3, -4, 2, -3, 1, -2, -1, 0):
        index = offset % N_Y
        xq_out[index] = chip_sum(1, offset, across).astype(BF)
        swapped[index] = go(
            xq_out.at[index], xq_in.at[index], sxq.at[index], rxq.at[index], partner
        )
    far = []
    for piece in range(2):
        lanes = slice(piece * FF, piece * FF + FF)
        far_out[piece] = chip_sum(0, 4, across, lanes).astype(BF)
        far.append(go(far_out.at[piece], far_in.at[piece], sfr.at[piece], rfr.at[piece], up_two))
        for way in range(2):
            reduce_step(piece, way, 0)
    for piece in range(2, 4):
        for way in range(2):
            reduce_step(piece, way, 0)
    ret[...] = (
        lax.dot_general(dhu_ref[...], w_mat[...], LAST, preferred_element_type=F32)
        .astype(BF).reshape(N_E, CAP, D)
    )
    back_rows = [
        go(ret.at[peer(k)], back.at[ex], sr.at[k], rr.at[k], (dp, peer(k)))
        for k in PEERS
    ]
    back_terms = [
        go(ret_s.at[peer(k)], back_s.at[ex], st.at[k], rt.at[k], (dp, peer(k)))
        for k in PEERS
    ]
    back[ex] = ret[ex]
    back_s[ex] = ret_s[ex]
    def ring_total(piece):
        total = own_term(piece, 0)
        for way in range(2):
            going[piece, way].wait_recv()
            total = total + recv_buf(piece, way, PARTS[piece][way] - 1)[...].astype(F32)
        return total

    crossing = []
    for step in range(4):
        if step == 3:
            for piece in range(2):
                xw_out[piece] = ring_total(piece).astype(BF)
                crossing.append(
                    go(xw_out.at[piece], xw_in.at[piece], sxr.at[piece], rxr.at[piece], partner)
                )
        for piece in range(4):
            for way in range(2):
                if 0 < step < PARTS[piece][way]:
                    reduce_step(piece, way, step)
        for way in range(2):
            if step < PARTS[4][way]:
                reduce_step(4, way, step)

    kept = [ring_total(2), ring_total(3)]
    wd_out[...] = ring_total(4).astype(BF)
    leave(4, wd_out, wd_out_hbm)

    for copy in back_rows + back_terms:
        copy.wait_recv()
    place = place_ref[...]
    tok_out[...] = lax.dot_general(
        place, back[...].reshape(SLOTS, D), ROWS, preferred_element_type=F32
    ).astype(BF)
    leave(0, tok_out, tok_hbm)
    terms = jnp.sum(
        jnp.where(diagonal[None], jnp.broadcast_to(back_s[...], (N_E, CAP, 128)), 0.0),
        axis=2, keepdims=True,
    )
    pick = (
        lax.broadcasted_iota(jnp.int32, (N_E, CAP, 128), 0)
        == lax.broadcasted_iota(jnp.int32, (N_E, CAP, 128), 2)
    )
    terms = jnp.where(pick, jnp.broadcast_to(terms, (N_E, CAP, 128)), 0.0)
    terms = terms.reshape(SLOTS, 128).astype(BF)
    by_expert = lax.dot_general(terms, place, ROWS, preferred_element_type=F32)[:N_E]
    ids = lax.broadcasted_iota(jnp.int32, (N_E, TOK), 0) * EXP_DEV
    line = lax.broadcasted_iota(jnp.int32, (8, TOK), 0)
    result = jnp.zeros((8, TOK), F32)
    route = routes[...]
    for k in range(8):
        value = jnp.sum(
            jnp.where(route[k : k + 1] == ids, by_expert, 0.0), axis=0, keepdims=True
        )
        result = jnp.where(line == k, value, result)
    gate_out[...] = result.astype(BF)
    leave(1, gate_out, gate_hbm)

    for piece, out in enumerate((wg_out, wu_out)):
        crossing[piece].wait_recv()
        out[...] = (kept[piece] + xw_in[piece].astype(F32)).astype(BF)
    leave(2, wg_out, wg_out_hbm)
    leave(3, wu_out, wu_out_hbm)
    for copy in leaving:
        copy.wait()
    for copy in started:
        copy.wait_send()


def hand_over(*refs):
    for i in range(5):
        refs[5 + i][...] = refs[i][...].reshape(refs[5 + i].shape)


def body(tokens, out_grad, routes, gate_values, w_gate, w_up, w_down):
    anywhere = pl.BlockSpec(memory_space=pl.ANY)
    vmem = pl.BlockSpec(memory_space=pltpu.VMEM)
    dma = pltpu.SemaphoreType.DMA
    shape = jax.ShapeDtypeStruct
    scratch = [
        pltpu.VMEM((TOK, D), BF),
        pltpu.VMEM((8, TOK), BF),
        pltpu.VMEM((UNIT, FF), BF),
        pltpu.VMEM((UNIT, FF), BF),
        pltpu.VMEM((DOWN, D), BF),
        pltpu.VMEM((TOK, D), BF),
        pltpu.VMEM((TOK, D), BF),
        pltpu.VMEM((8, TOK), jnp.int32),
        pltpu.VMEM((8, TOK), BF),
        pltpu.VMEM((SLOTS, TOK), BF),
        pltpu.VMEM((N_E, CAP, D), BF),
        pltpu.VMEM((N_E, CAP, D), BF),
        pltpu.VMEM((N_E, 1, 128), F32),
        pltpu.VMEM((N_E, CAP, D), BF),
        pltpu.VMEM((N_E, CAP, D), BF),
        pltpu.VMEM((N_E, 1, 128), F32),
        pltpu.VMEM((N_E, CAP, D), BF),
        pltpu.VMEM((N_E, CAP, D), BF),
        pltpu.VMEM((N_E, 1, 128), F32),
        pltpu.VMEM((N_E, 1, 128), F32),
        pltpu.VMEM((N_Y, 2, 2, UNIT, 2 * FF), BF),
        pltpu.VMEM((N_Y, 2, 2, DOWN, D), BF),
        pltpu.VMEM((D, 2 * FF), BF),
        pltpu.VMEM((D, SLOTS), BF),
        pltpu.VMEM((D, FF), BF),
        pltpu.VMEM((SLOTS, 2 * FF), F32),
        pltpu.VMEM((SLOTS, FF), F32),
        pltpu.VMEM((SLOTS, FF), BF),
        pltpu.VMEM((SLOTS, 2 * FF), BF),
        pltpu.VMEM((SLOTS, D), BF),
        pltpu.VMEM((N_Y, 2, 2, UNIT, 2 * FF), BF),
        pltpu.VMEM((N_Y, 2, 2, DOWN, D), BF),
        pltpu.VMEM((N_Y, 2, UNIT, 2 * FF), BF),
        pltpu.VMEM((N_Y, 2, DOWN, D), BF),
        pltpu.VMEM((4, 2, 4, UNIT, FF), BF),
        pltpu.VMEM((2, 4, DOWN, D), BF),
        pltpu.VMEM((4, 2, 4, UNIT, FF), BF),
        pltpu.VMEM((2, 4, DOWN, D), BF),
        pltpu.VMEM((N_Y, DOWN, D), BF),
        pltpu.VMEM((N_Y, DOWN, D), BF),
        pltpu.VMEM((2, UNIT, FF), BF),
        pltpu.VMEM((2, UNIT, FF), BF),
        pltpu.VMEM((2, UNIT, FF), BF),
        pltpu.VMEM((2, UNIT, FF), BF),
        dma((12,)),
        dma((N_E,)), dma((N_E,)), dma((N_E,)), dma((N_E,)),
        dma((N_E,)), dma((N_E,)), dma((N_E,)), dma((N_E,)),
        dma, dma,
        dma((N_Y,)), dma((N_Y,)),
        dma((3, 2, 4)), dma((3, 2, 4)),
        dma((4, N_Y)), dma((4, N_Y)),
        dma((2, N_Y)), dma((2, N_Y)),
        dma((5, 2, 4)), dma((5, 2, 4)),
        dma((N_Y,)), dma((N_Y,)),
        dma((2,)), dma((2,)),
        dma((2,)), dma((2,)),
        dma((N_E,)), dma((N_E,)),
    ]
    outs = pl.pallas_call(
        kernel,
        out_shape=(
            shape((TOK, D), BF), shape((8, TOK), BF),
            shape((UNIT, FF), BF), shape((UNIT, FF), BF), shape((DOWN, D), BF),
        ),
        in_specs=[anywhere] * 7,
        out_specs=(anywhere,) * 5,
        scratch_shapes=scratch,
        compiler_params=pltpu.CompilerParams(
            collective_id=0, has_side_effects=True, vmem_limit_bytes=60 * 1024 * 1024
        ),
    )(tokens, out_grad, routes.T, gate_values.T, w_gate, w_up, w_down)
    return pl.pallas_call(
        hand_over,
        out_shape=(
            shape((TOK, D), BF), shape((8, TOK), BF),
            shape((1, UNIT, FF), BF), shape((1, UNIT, FF), BF), shape((1, DOWN, D), BF),
        ),
        in_specs=[vmem] * 5,
        out_specs=(vmem,) * 5,
    )(*outs)


def solution(mesh):
    rows = P(("dp", "expert"), None)
    weight = P("expert", "dp", None)

    def whole(*args):
        token_grad, gate_grad, wg, wu, wd = body(*args)
        return token_grad, gate_grad.T, wg, wu, wd

    return jax.shard_map(
        whole,
        mesh=mesh,
        in_specs=(rows,) * 4 + (weight,) * 3,
        out_specs=(rows, rows, weight, weight, weight),
        check_vma=False,
    )
```
